32 devices in a mesh: tiles: 16 (over z, y, x), pix: 2 (over core).
Axes of the slice: x: 2, y: 2, z: 4, core: 2. Of those that a mesh axis runs over, the one named last changes fastest.
Arguments:
- frames: bfloat16 [4096, 8192], P('tiles', 'pix'), may hold values from -60 to 60
- tile_valid: int32 [4096], P('tiles'), may hold values from 0 to 1
- foreground_blocks: int32 [4096], P('tiles'), may hold values from 0 to 8, as said below
- basis_start: float32 [16, 8192], P(None, 'pix'), may hold values from -12 to 12
- dark_start: float32 [8192], P('pix'), may hold values from -4 to 4
Outputs:
- flatfield_basis: float32 [16, 8192], P(None, 'pix')
- darkfield: float32 [8192], P('pix')
- coefficients: float32 [4096, 16], P('tiles')
The draws below stay inside these ranges and needn't reach their ends.
Inputs may be any that keep to these rules, and one draw needn't show every extreme that they name: `foreground_blocks`: some tile has exactly 8.
All inputs are finite; a program needn't handle non-finite values.
Results may differ from the reference program's by a relative error of at most 0.0003.
Values sent between devices are 32-bit elements; how exact they have to be, the bound alone decides.
No kernel may reach another device: no remote copies, remote signals or barrier semaphores. Data moves between devices by JAX's collectives and lax.ppermute only.
A program may use at most 64 MiB of HBM per device.

```python
import math
import jax
import jax.numpy as jnp
from jax import lax

ROW_PX = 2048
RANK = 16
ITERS = 2
TILE_DEV = 256
NBLK = 16
PIXELS = 8192
TILES = 4096
N_TILES = 16


def masks_common(key):
    base = jax.random.fold_in(key, 101)
    usable = (jax.random.randint(jax.random.fold_in(base, 1), (TILES,), 0, 8) != 0).astype(jnp.int32)
    counts = jax.random.randint(jax.random.fold_in(base, 2), (TILES,), 0, NBLK // 2 + 1)
    chosen = jax.random.randint(jax.random.fold_in(base, 3), (), 0, TILES)
    counts = jnp.where(jnp.arange(TILES) == chosen, NBLK // 2, counts).astype(jnp.int32)
    return (usable, counts)


def factors_common(key):
    base = jax.random.fold_in(key, 202)
    latent = jax.random.normal(jax.random.fold_in(base, 1), (RANK, PIXELS), jnp.float32)
    image_scale = jnp.exp(jax.random.uniform(jax.random.fold_in(base, 2), (RANK, 1), jnp.float32, math.log(0.5), math.log(2.0)))
    pixel_basis = image_scale * (latent + 0.6 * latent[0:1])
    loads = jax.random.normal(jax.random.fold_in(base, 3), (TILES, RANK), jnp.float32)
    position = jnp.arange(TILES, dtype=jnp.float32) / TILES
    tile_scale = jnp.exp(math.log(3.0) * (position - 0.5))[:, None] * jnp.exp(jax.random.uniform(jax.random.fold_in(base, 4), (TILES, 1), jnp.float32, math.log(0.3), math.log(3.0)))
    tile_loads = tile_scale * (loads + 0.6 * loads[:, 0:1])
    return (tile_loads, pixel_basis, tile_scale)


def draw_frames(key, part):
    usable, counts = masks_common(key)
    tile_loads, pixel_basis, tile_scale = factors_common(key)
    base = jax.random.fold_in(key, 303)
    clean = jnp.zeros((TILES, PIXELS), jnp.float32)
    for index in range(RANK):
        clean = clean + tile_loads[:, index:index + 1] * pixel_basis[index:index + 1, :]
    noise = jax.random.truncated_normal(jax.random.fold_in(base, 1), -5.0, 5.0, (TILES, PIXELS), jnp.float32)
    place = jnp.arange(PIXELS, dtype=jnp.float32) / PIXELS
    pixel_scale = jnp.exp(math.log(3.0) * (place - 0.5)) * jnp.exp(jax.random.uniform(jax.random.fold_in(base, 2), (PIXELS,), jnp.float32, math.log(0.3), math.log(3.0)))
    true_dark = 0.5 * jax.random.truncated_normal(jax.random.fold_in(base, 3), -5.0, 5.0, (PIXELS,), jnp.float32)
    column = jnp.arange(PIXELS, dtype=jnp.int32) % ROW_PX // 128
    bright = (column[None, :] < counts[:, None]).astype(jnp.float32) * (3.0 + jax.random.truncated_normal(jax.random.fold_in(base, 4), -3.0, 3.0, (TILES, PIXELS), jnp.float32))
    garbage = 4.0 * jax.random.truncated_normal(jax.random.fold_in(base, 5), -5.0, 5.0, (TILES, PIXELS), jnp.float32)
    result = clean + true_dark[None, :] + 0.5 * tile_scale * pixel_scale[None, :] * noise + bright
    result = jnp.where(usable[:, None] == 1, result, garbage)
    return jnp.clip(result, -60.0, 60.0).astype(jnp.bfloat16)


def draw_tile_valid(key, part):
    return masks_common(key)[0]


def draw_foreground_blocks(key, part):
    return masks_common(key)[1]


def draw_basis_start(key, part):
    tile_loads, pixel_basis, tile_scale = factors_common(key)
    jitter = jax.random.normal(jax.random.fold_in(key, 404), (RANK, PIXELS), jnp.float32)
    return jnp.clip(pixel_basis + 0.3 * jitter, -12.0, 12.0)


def shard_levels(stream_key, shape, pieces, low, high):
    def one(axis_at, parts):
        draws = jax.random.uniform(jax.random.fold_in(jax.random.fold_in(stream_key, 6), axis_at), (parts,), jnp.float32, low / len(pieces), high / len(pieces))
        return jnp.repeat(jnp.exp(draws), shape[axis_at] // parts).reshape((-1,) + (1,) * (len(shape) - axis_at - 1))

    gain = one(*pieces[0])
    for cut in pieces[1:]:
        gain = gain * one(*cut)
    return gain


def scatter_about(key, extent, deviation, most, split=(), kind=jnp.bfloat16):
    values = jax.random.normal(key, extent, jnp.float32) * deviation
    if len(split) > 0:
        values = shard_levels(key, extent, split, -0.22, 0.18) * values
    return jnp.clip(values, min=-most, max=most).astype(kind)


def setup_inputs(seed: int = 0) -> dict:
    key_of = jax.random.split(jax.random.key(seed), 6)
    frames = draw_frames(jax.random.fold_in(key_of[5], 71), 0)
    tile_valid = draw_tile_valid(jax.random.fold_in(key_of[5], 71), 0)
    foreground_blocks = draw_foreground_blocks(jax.random.fold_in(key_of[5], 71), 0)
    basis_start = draw_basis_start(jax.random.fold_in(key_of[5], 71), 0)
    dark_start = scatter_about(key_of[4], (PIXELS,), 0.3, 4.0, ((0, 2),), jnp.float32)
    return dict(frames=frames, tile_valid=tile_valid, foreground_blocks=foreground_blocks, basis_start=basis_start, dark_start=dark_start)


precise = lax.Precision.HIGHEST
ridge_weight = 0.01

def solve_gram(gram_matrix, right_rows):
    factor = jnp.linalg.cholesky(gram_matrix)
    return jax.scipy.linalg.cho_solve((factor, True), right_rows)

def usable_mask(valid_rows, blocks_rows):
    column = jnp.arange(PIXELS, dtype=jnp.int32) % ROW_PX // 128
    return valid_rows[:, None].astype(jnp.float32) * (column[None, :] >= blocks_rows[:, None]).astype(jnp.float32)

def reference(frames, tile_valid, foreground_blocks, basis_start, dark_start):
    identity = jnp.eye(RANK, dtype=jnp.float32)
    frame_blocks = frames.reshape(N_TILES, TILE_DEV, PIXELS)
    valid_blocks = tile_valid.reshape(N_TILES, TILE_DEV)
    fore_blocks = foreground_blocks.reshape(N_TILES, TILE_DEV)
    basis = basis_start
    darkfield = dark_start
    coefficients = jnp.zeros((N_TILES, TILE_DEV, RANK), jnp.float32)
    for iteration in range(ITERS):
        gram_f = jnp.dot(basis, basis.T, precision=precise) / PIXELS + ridge_weight * identity

        def solve_block(packed):
            frame_rows, valid_rows, blocks_rows = packed
            shifted = frame_rows.astype(jnp.float32) - darkfield[None, :]
            projection = jnp.dot(shifted, basis.T, precision=precise) / PIXELS
            coef_rows = solve_gram(gram_f, projection.T).T
            residual = shifted - jnp.dot(coef_rows, basis, precision=precise)
            usable = usable_mask(valid_rows, blocks_rows)
            square_sum = jnp.sum(usable * residual * residual)
            valid_coef = coef_rows * valid_rows[:, None].astype(jnp.float32)
            coef_gram = jnp.dot(valid_coef.T, coef_rows, precision=precise)
            return (coef_rows, square_sum, coef_gram)
        coefficients, square_sums, coef_grams = lax.map(solve_block, (frame_blocks, valid_blocks, fore_blocks))
        spread = jnp.sum(square_sums) / (TILES * PIXELS) + 1e-05
        gram_c = jnp.sum(coef_grams, axis=0) / TILES + ridge_weight * identity

        def term_block(packed):
            frame_rows, valid_rows, blocks_rows, coef_rows = packed
            shifted = frame_rows.astype(jnp.float32) - darkfield[None, :]
            residual = shifted - jnp.dot(coef_rows, basis, precision=precise)
            usable = usable_mask(valid_rows, blocks_rows)
            weights = usable / (1.0 + residual * residual / (4.0 * spread))
            weighted = weights * residual
            return (jnp.dot(coef_rows.T, weighted, precision=precise), jnp.sum(weighted, axis=0), jnp.sum(weights, axis=0))
        basis_parts, dark_parts, weight_parts = lax.map(term_block, (frame_blocks, valid_blocks, fore_blocks, coefficients))
        basis_terms = jnp.sum(basis_parts, axis=0)
        dark_terms = jnp.sum(dark_parts, axis=0)
        weight_terms = jnp.sum(weight_parts, axis=0)
        basis = basis + solve_gram(gram_c, basis_terms / TILES)
        darkfield = darkfield + dark_terms / (weight_terms + 1.0)
    return (basis, darkfield, coefficients.reshape(TILES, RANK))
```

```python
import functools

import jax
import jax.numpy as jnp
from jax import lax
from jax.experimental import pallas as pl
from jax.experimental.pallas import tpu as pltpu
from jax.sharding import PartitionSpec as P

ROW_PX = 2048
BLOCK = 128
ITERS = 2
RIDGE = 0.01
VMEM_LIMIT = 48 * 1024 * 1024

F32 = jnp.float32
BF16 = jnp.bfloat16
NT = (((1,), (1,)), ((), ()))


def params():
    return pltpu.CompilerParams(vmem_limit_bytes=VMEM_LIMIT)


def vmem(n):
    return [pl.BlockSpec(memory_space=pltpu.VMEM)] * n


SMEM = pl.BlockSpec(memory_space=pltpu.SMEM)


def split3(x):
    hi = x.astype(BF16)
    rest = x - hi.astype(F32)
    mid = rest.astype(BF16)
    low = (rest - mid.astype(F32)).astype(BF16)
    return hi, mid, low


def eliminate(a, first, count):
    rows = lax.broadcasted_iota(jnp.int32, a.shape, 0)
    for k in range(count):
        column = a[:, first + k : first + k + 1]
        pivot = a[k : k + 1, first + k : first + k + 1]
        scaled = a[k : k + 1, :] * (1.0 / pivot)
        a = jnp.where(rows == k, scaled, a - column * scaled)
    return a


def eye_at(shape, first):
    row = lax.broadcasted_iota(jnp.int32, shape, 0)
    col = lax.broadcasted_iota(jnp.int32, shape, 1)
    return (col == row + first).astype(F32)


class Sizes:
    def __init__(self, tile_dev, pix_dev, rank, n_tiles, n_pix):
        self.tile_dev, self.pix_dev, self.rank = tile_dev, pix_dev, rank
        self.n_tiles, self.n_pix = n_tiles, n_pix
        self.tiles_all, self.pixels_all = tile_dev * n_tiles, pix_dev * n_pix
        self.tile_levels = levels(n_tiles)
        self.group = len(self.tile_levels[0]) + 1 if self.tile_levels else 1
        self.chunk = pix_dev // self.group
        self.blocks = self.chunk // BLOCK
        self.extra = BLOCK * (-(-2 * self.blocks // rank))
        self.stack = 6 * rank + 16


def levels(n):
    if n & (n - 1):
        return None
    out, bit = [], 1
    while bit < n:
        out.append((bit, 2 * bit, 3 * bit) if 4 * bit <= n else (bit,))
        bit *= 4
    return out


def partner(x, axis, mask):
    n = lax.axis_size(axis)
    return lax.ppermute(x, axis, [(i, i ^ mask) for i in range(n)])


def tree(parts):
    while len(parts) > 1:
        parts = [a + b for a, b in zip(parts[::2], parts[1::2])]
    return parts[0]


def sum_level(x, axis, masks):
    return tree([x] + [partner(x, axis, m) for m in masks])


def stack_block(sz, stack_ref, offset, b, d_rows):
    r = sz.rank
    hi, mid, low = split3(b)
    span = pl.ds(offset, b.shape[1])
    for at, part in enumerate((hi, mid, low, hi, mid, hi)):
        stack_ref[at * r : (at + 1) * r, span] = part
    for j, d in enumerate(d_rows):
        at = pl.ds(offset + j * BLOCK, BLOCK)
        d_hi, d_mid, d_low = split3(d)
        row = lax.broadcasted_iota(jnp.int32, (16, BLOCK), 0)
        tile = jnp.where(
            row == 0,
            d_hi.astype(F32),
            jnp.where(row == 1, d_mid.astype(F32), jnp.where(row == 2, d_low.astype(F32), 0.0)),
        )
        stack_ref[6 * r : 6 * r + 16, at] = tile.astype(BF16)


def project_chunk(sz, f_ref, stack_ref, offset, b, d_rows, totals):
    r = sz.rank
    stack_block(sz, stack_ref, offset, b, d_rows)
    span = pl.ds(offset, b.shape[1])
    parts = stack_ref[0 : 3 * r, span]
    proj = lax.dot_general(parts, f_ref[:, span], NT, preferred_element_type=F32)
    gram = lax.dot_general(parts, parts, NT, preferred_element_type=F32)
    dark = None
    for j, d in enumerate(d_rows):
        term = b[:, j * BLOCK : (j + 1) * BLOCK] * d
        dark = term if dark is None else dark + term
    new = (proj, gram, dark)
    return new if totals is None else tuple(a + b for a, b in zip(totals, new))


def pack_projections(sz, totals, packed_ref):
    r, td = sz.rank, sz.tile_dev
    proj, gram, dark = totals
    proj = proj[0:r] + proj[r : 2 * r] + proj[2 * r : 3 * r]
    gram = gram[0:r] + gram[r : 2 * r] + gram[2 * r : 3 * r]
    gram = gram[:, 0:r] + gram[:, r : 2 * r] + gram[:, 2 * r : 3 * r]
    packed_ref[:, 0:td] = proj - jnp.sum(dark, axis=1, keepdims=True)
    packed_ref[:, td : td + BLOCK] = jnp.zeros((r, BLOCK), F32)
    packed_ref[:, td : td + r] = gram


def first_projection(sz, me_ref, f_ref, b_ref, d_ref, valid_ref, fore_ref, packed_ref, stack_ref, own_ref, least_ref):
    totals = None
    for c in range(sz.group):
        at = c * sz.chunk
        d_rows = [d_ref[c * sz.blocks + j : c * sz.blocks + j + 1, :] for j in range(sz.blocks)]
        totals = project_chunk(sz, f_ref, stack_ref, at, b_ref[:, at : at + sz.chunk], d_rows, totals)
    pack_projections(sz, totals, packed_ref)
    me = me_ref[0]
    own_ref[:, 0 : sz.chunk] = b_ref[:, pl.ds(pl.multiple_of(me * sz.chunk, BLOCK), sz.chunk)]
    own_ref[:, sz.chunk :] = jnp.zeros((sz.rank, sz.extra), F32)
    for j in range(sz.blocks):
        own_ref[j % sz.rank, pl.ds(sz.chunk + j // sz.rank * BLOCK, BLOCK)] = d_ref[me * sz.blocks + j, :]
    least = jnp.where(valid_ref[...] != 0, fore_ref[...], ROW_PX)
    least_ref[...] = jnp.broadcast_to(least, (BLOCK, sz.tile_dev)).T


def later_projection(sz, me_ref, f_ref, *refs):
    chunks, (packed_ref, stack_ref) = refs[: sz.group], refs[sz.group :]
    me = me_ref[0]
    totals = None
    for k, ref in enumerate(chunks):
        at = pl.multiple_of((me ^ k) * sz.chunk, BLOCK)
        d_rows = [
            ref[j % sz.rank : j % sz.rank + 1, sz.chunk + j // sz.rank * BLOCK : sz.chunk + (j // sz.rank + 1) * BLOCK]
            for j in range(sz.blocks)
        ]
        totals = project_chunk(sz, f_ref, stack_ref, at, ref[:, 0 : sz.chunk], d_rows, totals)
    pack_projections(sz, totals, packed_ref)


def residual(sz, f_ref, stack_ref, parts, offset, width):
    span = pl.ds(offset, width)
    model = lax.dot_general(
        parts, stack_ref[:, span], (((1,), (0,)), ((), ())), preferred_element_type=F32
    )
    return f_ref[:, span].astype(F32) - model


def solve_tiles(sz, width, *refs):
    packed = refs[: sz.n_pix]
    f_ref, stack_ref, least_ref, valid_ref, coef_ref, parts_ref, note_ref = refs[sz.n_pix :]
    r, td = sz.rank, sz.tile_dev
    a = tree([ref[...] for ref in packed]) / sz.pixels_all
    a = a + RIDGE * eye_at(a.shape, td)
    coef = eliminate(a, td, r)[:, 0:td]
    coef_ref[...] = coef
    hi, mid, low = split3(coef)
    row = lax.broadcasted_iota(jnp.int32, (BLOCK - 6 * r, td), 0)
    ones = (row < 3).astype(F32)
    hi, mid, low = hi.astype(F32), mid.astype(F32), low.astype(F32)
    parts = jnp.concatenate([hi, hi, hi, mid, mid, low, ones], axis=0).T.astype(BF16)
    parts_ref[...] = parts
    parts = parts[:, 0 : sz.stack]
    least = least_ref[...]

    def body(step, total):
        offset = pl.multiple_of(step * width, BLOCK)
        res = residual(sz, f_ref, stack_ref, parts, offset, width)
        square = res * res
        for j in range(width // BLOCK):
            block = (step * (width // BLOCK) + j) % (ROW_PX // BLOCK)
            term = jnp.where(least <= block, square[:, j * BLOCK : (j + 1) * BLOCK], 0.0)
            total = total + jnp.sum(term.reshape(td // 8, 8, BLOCK), axis=0)
        return total

    total = lax.fori_loop(0, sz.pix_dev // width, body, jnp.zeros((8, BLOCK), F32))
    total = jnp.sum(jnp.sum(total, axis=0, keepdims=True), axis=1, keepdims=True)
    held = coef * (valid_ref[...] != 0).astype(F32)
    gram = lax.dot_general(held, coef, NT, precision=lax.Precision.HIGHEST, preferred_element_type=F32)
    note_ref[...] = jnp.zeros((r, BLOCK), F32)
    note_ref[:, 0:r] = gram
    note_ref[0:1, r : r + 1] = total


def invert_gram(sz, note_ref, inverse_ref):
    r = sz.rank
    gram = note_ref[:, 0:r] / sz.tiles_all + RIDGE * eye_at((r, r), 0)
    a = jnp.concatenate([gram, eye_at((r, BLOCK - r), 0)], axis=1)
    inverse_ref[...] = eliminate(a, 0, r)


def update_terms(sz, width, me_ref, *refs):
    notes = refs[: sz.n_pix]
    f_ref, stack_ref, least_ref, coef_ref, parts_ref = refs[sz.n_pix : sz.n_pix + 5]
    outs = refs[sz.n_pix + 5 :]
    r, td = sz.rank, sz.tile_dev
    me = me_ref[0]
    total = tree([ref[0:1, r : r + 1] for ref in notes])
    spread = total / (sz.tiles_all * sz.pixels_all) + 1e-05
    scale = jnp.broadcast_to(1.0 / (4.0 * spread), (8, BLOCK))[0:1, :]
    parts = parts_ref[:, 0 : sz.stack]
    hi, mid, low = split3(coef_ref[...])
    three = jnp.concatenate([hi, mid, low], axis=0)
    least = least_ref[...]
    steps = sz.chunk // width
    for k, out_ref in enumerate(outs):
        start = (me ^ k) * sz.chunk
        for step in range(steps):
            offset = pl.multiple_of(start + step * width, BLOCK)
            res = residual(sz, f_ref, stack_ref, parts, offset, width)
            hi_parts, mid_parts = [], []
            for j in range(width // BLOCK):
                block = (offset // BLOCK + j) % (ROW_PX // BLOCK)
                x = res[:, j * BLOCK : (j + 1) * BLOCK]
                t = x * x * scale + 1.0
                g = pl.reciprocal(t, approx=True)
                g = g * (2.0 - t * g)
                g = jnp.where(least <= block, g, 0.0)
                w = g * x
                w_hi = w.astype(BF16)
                hi_parts.append(w_hi)
                mid_parts.append((w - w_hi.astype(F32)).astype(BF16))
                at = step * (width // BLOCK) + j
                for flat, value in ((at, w), (sz.blocks + at, g)):
                    lane = sz.chunk + flat // r * BLOCK
                    out_ref[flat % r : flat % r + 1, lane : lane + BLOCK] = jnp.sum(value, axis=0, keepdims=True)
            nn = (((1,), (0,)), ((), ()))
            terms = lax.dot_general(three, jnp.concatenate(hi_parts, axis=1), nn, preferred_element_type=F32)
            more = lax.dot_general(three[0 : 2 * r], jnp.concatenate(mid_parts, axis=1), nn, preferred_element_type=F32)
            out_ref[:, step * width : (step + 1) * width] = (
                terms[0:r] + (terms[r : 2 * r] + terms[2 * r : 3 * r] + more[0:r] + more[r : 2 * r])
            )
    used = 2 * sz.blocks
    if used % r:
        for out_ref in outs:
            out_ref[used % r :, sz.chunk + used // r * BLOCK :] = jnp.zeros((r - used % r, BLOCK), F32)


def update_chunk(sz, inverse_ref, old_ref, *refs):
    total_refs, new_ref = refs[:-1], refs[-1]
    r = sz.rank
    totals = tree([ref[...] for ref in total_refs])
    inverse = inverse_ref[:, r : 2 * r]
    change = jnp.dot(inverse, totals[:, 0 : sz.chunk] / sz.tiles_all, precision=lax.Precision.HIGHEST, preferred_element_type=F32)
    new_ref[:, 0 : sz.chunk] = old_ref[:, 0 : sz.chunk] + change
    new_ref[:, sz.chunk :] = jnp.zeros((r, sz.extra), F32)

    def place(flat):
        return flat % r, sz.chunk + flat // r * BLOCK

    many = 8 if sz.blocks % 8 == 0 else 1
    for j in range(0, sz.blocks, many):
        (row, lane), (row_g, lane_g) = place(j), place(sz.blocks + j)
        w = totals[row : row + many, lane : lane + BLOCK]
        g = totals[row_g : row_g + many, lane_g : lane_g + BLOCK]
        new_ref[row : row + many, lane : lane + BLOCK] = (
            old_ref[row : row + many, lane : lane + BLOCK] + w / (g + 1.0)
        )


def assemble(sz, me_ref, *refs):
    chunks, (b_ref, d_ref) = refs[: sz.group], refs[sz.group :]
    me = me_ref[0]
    for k, ref in enumerate(chunks):
        c = me ^ k
        b_ref[:, pl.ds(pl.multiple_of(c * sz.chunk, BLOCK), sz.chunk)] = ref[:, 0 : sz.chunk]
        for j in range(sz.blocks):
            lane = sz.chunk + j // sz.rank * BLOCK
            d_ref[c * sz.blocks + j, :] = ref[j % sz.rank, lane : lane + BLOCK]


def call(body, outs, ins, smem=0, cost=None):
    return pl.pallas_call(
        body,
        out_shape=[jax.ShapeDtypeStruct(s, t) for s, t in outs],
        in_specs=[SMEM] * smem + vmem(len(ins) - smem),
        out_specs=vmem(len(outs)),
        compiler_params=params(),
    )(*ins)


def local(frames, tile_valid, foreground_blocks, basis_start, dark_start):
    td, pd = frames.shape
    r = basis_start.shape[0]
    sz = Sizes(td, pd, r, lax.axis_size("tiles"), lax.axis_size("pix"))
    pix_masks = [m for m in range(1, sz.n_pix)]
    me = (lax.axis_index("tiles") & (sz.group - 1)).astype(jnp.int32).reshape(1)
    valid = tile_valid.reshape(1, td)
    fore = foreground_blocks.reshape(1, td)
    width = min(512, sz.chunk)
    chunk_shape = (r, sz.chunk + sz.extra)
    packed_out = ((r, td + BLOCK), F32)
    stack_out = ((sz.stack, pd), BF16)
    masks = sz.tile_levels[0]
    for iteration in range(ITERS):
        if iteration == 0:
            packed, stack, old, least = call(
                functools.partial(first_projection, sz),
                [packed_out, stack_out, (chunk_shape, F32), ((td, BLOCK), jnp.int32)],
                [me, frames, basis_start, dark_start.reshape(pd // BLOCK, BLOCK), valid, fore],
                smem=1,
            )
        else:
            packed, stack = call(
                functools.partial(later_projection, sz), [packed_out, stack_out], [me, frames] + chunks, smem=1
            )
        both = [packed] + [partner(packed, "pix", m) for m in pix_masks]
        coef, parts, note = call(
            functools.partial(solve_tiles, sz, width),
            [((r, td), F32), ((td, BLOCK), BF16), ((r, BLOCK), F32)],
            both + [frames, stack, least, valid],
        )
        for level in sz.tile_levels:
            note = sum_level(note, "tiles", level)
        (inverse,) = call(functools.partial(invert_gram, sz), [((r, BLOCK), F32)], [note])
        notes = [note] + [partner(note, "pix", m) for m in pix_masks]
        terms = call(
            functools.partial(update_terms, sz, width),
            [(chunk_shape, F32)] * sz.group,
            [me] + notes + [frames, stack, least, coef, parts],
            smem=1,
        )
        total = tree([terms[0]] + [partner(terms[k], "tiles", m) for k, m in enumerate(masks, 1)])
        later = sz.tile_levels[1:]
        for level in later[:-1]:
            total = sum_level(total, "tiles", level)
        totals = [total] + [partner(total, "tiles", m) for m in (later[-1] if later else ())]
        (old,) = call(functools.partial(update_chunk, sz), [(chunk_shape, F32)], [inverse, old] + totals)
        chunks = [old] + [partner(old, "tiles", m) for m in masks]
    basis, dark = call(
        functools.partial(assemble, sz), [((r, pd), F32), ((pd // BLOCK, BLOCK), F32)], [me] + chunks, smem=1
    )
    return basis, dark.reshape(pd), coef.T


def solution(mesh):
    return jax.shard_map(
        local,
        mesh=mesh,
        in_specs=(P("tiles", "pix"), P("tiles"), P("tiles"), P(None, "pix"), P("pix")),
        out_specs=(P(None, "pix"), P("pix"), P("tiles", None)),
        check_vma=False,
    )
```

```python
import functools

import jax
import jax.numpy as jnp
from jax import lax
from jax.experimental import pallas as pl
from jax.experimental.pallas import tpu as pltpu
from jax.sharding import PartitionSpec as P

ROW_PX = 2048
BLOCK = 128
ITERS = 2
RIDGE = 0.01
VMEM_LIMIT = 48 * 1024 * 1024

F32 = jnp.float32
BF16 = jnp.bfloat16
NT = (((1,), (1,)), ((), ()))


def params():
    return pltpu.CompilerParams(vmem_limit_bytes=VMEM_LIMIT)


def vmem(n):
    return [pl.BlockSpec(memory_space=pltpu.VMEM)] * n


SMEM = pl.BlockSpec(memory_space=pltpu.SMEM)


def split3(x):
    hi = x.astype(BF16)
    rest = x - hi.astype(F32)
    mid = rest.astype(BF16)
    low = (rest - mid.astype(F32)).astype(BF16)
    return hi, mid, low


def solve_spd(gram, sides):
    r = gram.shape[0]
    columns = [jnp.broadcast_to(gram[:, j : j + 1], (r, BLOCK)) for j in range(r)]
    rows = lax.broadcasted_iota(jnp.int32, (r, BLOCK), 0)
    for k in range(r):
        pivot = columns[k]
        inverse = 1.0 / pivot[k : k + 1, :]

        def step(x):
            scaled = x[k : k + 1, :] * inverse
            return jnp.where(rows == k, scaled, x - pivot * scaled)

        columns = columns[: k + 1] + [step(c) for c in columns[k + 1 :]]
        sides = [step(x) for x in sides]
    return sides


def eye_at(shape, first):
    row = lax.broadcasted_iota(jnp.int32, shape, 0)
    col = lax.broadcasted_iota(jnp.int32, shape, 1)
    return (col == row + first).astype(F32)


class Sizes:
    def __init__(self, tile_dev, pix_dev, rank, n_tiles, n_pix):
        self.tile_dev, self.pix_dev, self.rank = tile_dev, pix_dev, rank
        self.n_tiles, self.n_pix = n_tiles, n_pix
        self.tiles_all, self.pixels_all = tile_dev * n_tiles, pix_dev * n_pix
        self.tile_levels = levels(n_tiles)
        self.group = len(self.tile_levels[0]) + 1 if self.tile_levels else 1
        self.chunk = pix_dev // self.group
        self.blocks = self.chunk // BLOCK
        self.extra = BLOCK * (-(-2 * self.blocks // rank))
        self.stack = 6 * rank + 16
        self.spot, self.twin = rank * rank - 2, rank * rank - rank - 1


def levels(n):
    if n & (n - 1):
        return None
    out, bit = [], 1
    while bit < n:
        out.append((bit, 2 * bit, 3 * bit) if 4 * bit <= n else (bit,))
        bit *= 4
    return out


def partner(x, axis, mask):
    n = lax.axis_size(axis)
    return lax.ppermute(x, axis, [(i, i ^ mask) for i in range(n)])


def tree(parts):
    while len(parts) > 1:
        parts = [a + b for a, b in zip(parts[::2], parts[1::2])]
    return parts[0]


def sum_level(x, axis, masks):
    return tree([x] + [partner(x, axis, m) for m in masks])


def stack_block(sz, stack_ref, offset, b, d_rows):
    r = sz.rank
    hi, mid, low = split3(b)
    span = pl.ds(offset, b.shape[1])
    for at, part in enumerate((hi, mid, low, hi, mid, hi)):
        stack_ref[at * r : (at + 1) * r, span] = part
    for j, d in enumerate(d_rows):
        at = pl.ds(offset + j * BLOCK, BLOCK)
        d_hi, d_mid, d_low = split3(d)
        row = lax.broadcasted_iota(jnp.int32, (16, BLOCK), 0)
        tile = jnp.where(
            row == 0,
            d_hi.astype(F32),
            jnp.where(row == 1, d_mid.astype(F32), jnp.where(row == 2, d_low.astype(F32), 0.0)),
        )
        stack_ref[6 * r : 6 * r + 16, at] = tile.astype(BF16)


def project_chunk(sz, f_ref, stack_ref, offset, b, d_rows, totals):
    r = sz.rank
    stack_block(sz, stack_ref, offset, b, d_rows)
    span = pl.ds(offset, b.shape[1])
    parts = stack_ref[0 : 3 * r, span]
    proj = lax.dot_general(parts, f_ref[:, span], NT, preferred_element_type=F32)
    gram = lax.dot_general(parts, parts, NT, preferred_element_type=F32)
    dark = None
    for j, d in enumerate(d_rows):
        term = b[:, j * BLOCK : (j + 1) * BLOCK] * d
        dark = term if dark is None else dark + term
    new = (proj, gram, dark)
    return new if totals is None else tuple(a + b for a, b in zip(totals, new))


def pack_projections(sz, totals, packed_ref):
    r, td = sz.rank, sz.tile_dev
    proj, gram, dark = totals
    proj = proj[0:r] + proj[r : 2 * r] + proj[2 * r : 3 * r]
    gram = gram[0:r] + gram[r : 2 * r] + gram[2 * r : 3 * r]
    gram = gram[:, 0:r] + gram[:, r : 2 * r] + gram[:, 2 * r : 3 * r]
    packed_ref[:, 0:td] = proj - jnp.sum(dark, axis=1, keepdims=True)
    packed_ref[:, td : td + BLOCK] = jnp.zeros((r, BLOCK), F32)
    packed_ref[:, td : td + r] = gram


def first_projection(sz, f_hbm, b_hbm, d_hbm, valid_hbm, fore_hbm, f_ref, packed_ref, stack_ref, own_ref, least_ref, valid_ref, b_ref, d_ref, flags_ref, sems):
    small = [
        pltpu.make_async_copy(d_hbm, d_ref, sems.at[0]),
        pltpu.make_async_copy(b_hbm, b_ref, sems.at[1]),
        pltpu.make_async_copy(valid_hbm, flags_ref.at[0:1], sems.at[2]),
        pltpu.make_async_copy(fore_hbm, flags_ref.at[8:9], sems.at[3]),
    ]
    spans = [pl.ds(c * sz.chunk, sz.chunk) for c in range(sz.group)]
    large = [pltpu.make_async_copy(f_hbm.at[:, s], f_ref.at[:, s], sems.at[4 + c]) for c, s in enumerate(spans)]
    for copy in small + large:
        copy.start()
    for copy in small:
        copy.wait()
    valid = flags_ref[0:1, :] != 0
    valid_ref[...] = jnp.broadcast_to(valid.astype(F32), valid_ref.shape)
    least_ref[...] = jnp.broadcast_to(jnp.where(valid, flags_ref[8:9, :], ROW_PX), (BLOCK, sz.tile_dev)).T
    me = lax.axis_index("tiles") & (sz.group - 1)
    own_ref[:, 0 : sz.chunk] = b_ref[:, pl.ds(pl.multiple_of(me * sz.chunk, BLOCK), sz.chunk)]
    own_ref[:, sz.chunk :] = jnp.zeros((sz.rank, sz.extra), F32)
    for j in range(sz.blocks):
        own_ref[j % sz.rank, pl.ds(sz.chunk + j // sz.rank * BLOCK, BLOCK)] = d_ref[me * sz.blocks + j, :]
    totals = None
    for c in range(sz.group):
        at = c * sz.chunk
        large[c].wait()
        d_rows = [d_ref[c * sz.blocks + j : c * sz.blocks + j + 1, :] for j in range(sz.blocks)]
        totals = project_chunk(sz, f_ref, stack_ref, at, b_ref[:, at : at + sz.chunk], d_rows, totals)
    pack_projections(sz, totals, packed_ref)


def later_projection(sz, f_ref, *refs):
    chunks, (packed_ref, stack_ref) = refs[: sz.group], refs[sz.group :]
    me = lax.axis_index("tiles") & (sz.group - 1)
    totals = None
    for k, ref in enumerate(chunks):
        at = pl.multiple_of((me ^ k) * sz.chunk, BLOCK)
        d_rows = [
            ref[j % sz.rank : j % sz.rank + 1, sz.chunk + j // sz.rank * BLOCK : sz.chunk + (j // sz.rank + 1) * BLOCK]
            for j in range(sz.blocks)
        ]
        totals = project_chunk(sz, f_ref, stack_ref, at, ref[:, 0 : sz.chunk], d_rows, totals)
    pack_projections(sz, totals, packed_ref)


def residual(sz, f_ref, stack_ref, parts, offset, width):
    span = pl.ds(offset, width)
    model = lax.dot_general(
        parts, stack_ref[:, span], (((1,), (0,)), ((), ())), preferred_element_type=F32
    )
    return f_ref[:, span].astype(F32) - model


def solve_tiles(sz, width, *refs):
    packed = refs[: sz.n_pix]
    f_ref, stack_ref, least_ref, valid_ref, coef_ref, parts_ref, note_ref = refs[sz.n_pix :]
    r, td = sz.rank, sz.tile_dev
    a = tree([ref[...] for ref in packed]) / sz.pixels_all
    gram = a[:, td : td + r] + RIDGE * eye_at((r, r), 0)
    sides = [a[:, at : at + BLOCK] for at in range(0, td, BLOCK)]
    coef = jnp.concatenate(solve_spd(gram, sides), axis=1)
    coef_ref[...] = coef
    hi, mid, low = split3(coef)
    row = lax.broadcasted_iota(jnp.int32, (BLOCK - 6 * r, td), 0)
    ones = (row < 3).astype(F32)
    hi, mid, low = hi.astype(F32), mid.astype(F32), low.astype(F32)
    parts = jnp.concatenate([hi, hi, hi, mid, mid, low, ones], axis=0).T.astype(BF16)
    parts_ref[...] = parts
    parts = parts[:, 0 : sz.stack]
    least = least_ref[...]

    total = jnp.zeros((8, BLOCK), F32)
    for offset in range(0, sz.pix_dev, width):
        res = residual(sz, f_ref, stack_ref, parts, offset, width)
        square = res * res
        for j in range(width // BLOCK):
            block = (offset // BLOCK + j) % (ROW_PX // BLOCK)
            term = jnp.where(least <= block, square[:, j * BLOCK : (j + 1) * BLOCK], 0.0)
            total = total + jnp.sum(term.reshape(td // 8, 8, BLOCK), axis=0)
    total = jnp.sum(jnp.sum(total, axis=0, keepdims=True), axis=1, keepdims=True)
    products = jnp.concatenate([coef[i : i + 1] * coef for i in range(r)], axis=0)
    ones = valid_ref[...].astype(BF16)
    flat = sum(lax.dot_general(ones, part, NT, preferred_element_type=F32) for part in split3(products))
    lane = lax.broadcasted_iota(jnp.int32, flat.shape, 1)
    flat = jnp.where(lane == sz.spot, total, flat)
    for at in range(0, note_ref.shape[0], 8):
        note_ref[at : at + 8, :] = flat


def invert_gram(sz, note_ref, inverse_ref):
    r = sz.rank
    flat = jnp.sum(note_ref[...], axis=0, keepdims=True)
    gram = jnp.concatenate([flat[:, i * r : (i + 1) * r] for i in range(r)], axis=0)
    row = lax.broadcasted_iota(jnp.int32, (r, r), 0)
    col = lax.broadcasted_iota(jnp.int32, (r, r), 1)
    twin = flat[:, sz.twin : sz.twin + 1]
    gram = jnp.where((row == r - 1) & (col == r - 2), twin, gram)
    gram = gram / (sz.n_pix * sz.tiles_all) + RIDGE * eye_at((r, r), 0)
    (inverse_ref[...],) = solve_spd(gram, [eye_at((r, BLOCK), 0)])


def update_terms(sz, width, note_ref, f_ref, stack_ref, least_ref, coef_ref, parts_ref, *outs):
    r, td = sz.rank, sz.tile_dev
    me = lax.axis_index("tiles") & (sz.group - 1)
    total = jnp.sum(note_ref[:, sz.spot : sz.spot + 1], axis=0, keepdims=True)
    spread = total / (sz.tiles_all * sz.pixels_all) + 1e-05
    scale = jnp.broadcast_to(1.0 / (4.0 * spread), (8, BLOCK))[0:1, :]
    parts = parts_ref[:, 0 : sz.stack]
    hi, mid, low = split3(coef_ref[...])
    three = jnp.concatenate([hi, mid, low], axis=0)
    least = least_ref[...]
    steps = sz.chunk // width
    for k, out_ref in enumerate(outs):
        start = (me ^ k) * sz.chunk
        for step in range(steps):
            offset = pl.multiple_of(start + step * width, BLOCK)
            res = residual(sz, f_ref, stack_ref, parts, offset, width)
            hi_parts, mid_parts = [], []
            for j in range(width // BLOCK):
                block = (offset // BLOCK + j) % (ROW_PX // BLOCK)
                x = res[:, j * BLOCK : (j + 1) * BLOCK]
                t = x * x * scale + 1.0
                g = pl.reciprocal(t, approx=True)
                g = g * (2.0 - t * g)
                g = jnp.where(least <= block, g, 0.0)
                w = g * x
                w_hi = w.astype(BF16)
                hi_parts.append(w_hi)
                mid_parts.append((w - w_hi.astype(F32)).astype(BF16))
                at = step * (width // BLOCK) + j
                for flat, value in ((at, w), (sz.blocks + at, g)):
                    lane = sz.chunk + flat // r * BLOCK
                    out_ref[flat % r : flat % r + 1, lane : lane + BLOCK] = jnp.sum(value, axis=0, keepdims=True)
            nn = (((1,), (0,)), ((), ()))
            terms = lax.dot_general(three, jnp.concatenate(hi_parts, axis=1), nn, preferred_element_type=F32)
            more = lax.dot_general(three[0 : 2 * r], jnp.concatenate(mid_parts, axis=1), nn, preferred_element_type=F32)
            out_ref[:, step * width : (step + 1) * width] = (
                terms[0:r] + (terms[r : 2 * r] + terms[2 * r : 3 * r] + more[0:r] + more[r : 2 * r])
            )
    used = 2 * sz.blocks
    if used % r:
        for out_ref in outs:
            out_ref[used % r :, sz.chunk + used // r * BLOCK :] = jnp.zeros((r - used % r, BLOCK), F32)


def update_chunk(sz, inverse_ref, old_ref, *refs):
    total_refs, new_ref = refs[:-1], refs[-1]
    r = sz.rank
    totals = tree([ref[...] for ref in total_refs])
    inverse = inverse_ref[:, 0:r]
    change = jnp.dot(inverse, totals[:, 0 : sz.chunk] / sz.tiles_all, precision=lax.Precision.HIGHEST, preferred_element_type=F32)
    new_ref[:, 0 : sz.chunk] = old_ref[:, 0 : sz.chunk] + change
    new_ref[:, sz.chunk :] = jnp.zeros((r, sz.extra), F32)

    def place(flat):
        return flat % r, sz.chunk + flat // r * BLOCK

    many = 8 if sz.blocks % 8 == 0 else 1
    for j in range(0, sz.blocks, many):
        (row, lane), (row_g, lane_g) = place(j), place(sz.blocks + j)
        w = totals[row : row + many, lane : lane + BLOCK]
        g = totals[row_g : row_g + many, lane_g : lane_g + BLOCK]
        new_ref[row : row + many, lane : lane + BLOCK] = (
            old_ref[row : row + many, lane : lane + BLOCK] + w / (g + 1.0)
        )


def assemble(sz, *refs):
    chunks, (b_ref, d_ref) = refs[: sz.group], refs[sz.group :]
    me = lax.axis_index("tiles") & (sz.group - 1)
    for k, ref in enumerate(chunks):
        c = me ^ k
        b_ref[:, pl.ds(pl.multiple_of(c * sz.chunk, BLOCK), sz.chunk)] = ref[:, 0 : sz.chunk]
        for j in range(sz.blocks):
            lane = sz.chunk + j // sz.rank * BLOCK
            d_ref[c * sz.blocks + j, :] = ref[j % sz.rank, lane : lane + BLOCK]


def call(body, outs, ins, in_hbm=False, scratch=()):
    return pl.pallas_call(
        body,
        out_shape=[jax.ShapeDtypeStruct(s, t) for s, t in outs],
        in_specs=[pl.BlockSpec(memory_space=pltpu.HBM)] * len(ins) if in_hbm else vmem(len(ins)),
        out_specs=vmem(len(outs)),
        scratch_shapes=scratch,
        compiler_params=params(),
    )(*([pltpu.with_memory_space_constraint(x, pltpu.HBM) for x in ins] if in_hbm else ins))


def local(frames, tile_valid, foreground_blocks, basis_start, dark_start):
    td, pd = frames.shape
    r = basis_start.shape[0]
    sz = Sizes(td, pd, r, lax.axis_size("tiles"), lax.axis_size("pix"))
    everyone = ("tiles", "pix")
    devices = sz.n_tiles * sz.n_pix
    pix_masks = range(1, sz.n_pix)
    width = min(512, sz.chunk)
    chunk_shape = (r, sz.chunk + sz.extra)
    packed_out = ((r, td + BLOCK), F32)
    stack_out = ((sz.stack, pd), BF16)
    masks = sz.tile_levels[0]
    for iteration in range(ITERS):
        if iteration == 0:
            frames, packed, stack, old, least, valid = call(
                functools.partial(first_projection, sz),
                [((td, pd), BF16), packed_out, stack_out, (chunk_shape, F32), ((td, BLOCK), jnp.int32), ((8, td), F32)],
                [frames, basis_start, dark_start.reshape(pd // BLOCK, BLOCK), tile_valid.reshape(1, td), foreground_blocks.reshape(1, td)],
                in_hbm=True,
                scratch=[
                    pltpu.VMEM((r, pd), F32),
                    pltpu.VMEM((pd // BLOCK, BLOCK), F32),
                    pltpu.VMEM((16, td), jnp.int32),
                    pltpu.SemaphoreType.DMA((4 + sz.group,)),
                ],
            )
        else:
            packed, stack = call(functools.partial(later_projection, sz), [packed_out, stack_out], [frames] + chunks)
        both = [packed] + [partner(packed, "pix", m) for m in pix_masks]
        coef, parts, note = call(
            functools.partial(solve_tiles, sz, width),
            [((r, td), F32), ((td, BLOCK), BF16), ((devices, r * r), F32)],
            both + [frames, stack, least, valid],
        )
        notes = lax.all_to_all(note, everyone, 0, 0, tiled=True)
        (inverse,) = call(functools.partial(invert_gram, sz), [((r, BLOCK), F32)], [notes])
        terms = call(
            functools.partial(update_terms, sz, width),
            [(chunk_shape, F32)] * sz.group,
            [notes, frames, stack, least, coef, parts],
        )
        total = tree([terms[0]] + [partner(terms[k], "tiles", m) for k, m in enumerate(masks, 1)])
        later = sz.tile_levels[1:]
        for level in later[:-1]:
            total = sum_level(total, "tiles", level)
        totals = [total] + [partner(total, "tiles", m) for m in (later[-1] if later else ())]
        (old,) = call(functools.partial(update_chunk, sz), [(chunk_shape, F32)], [inverse, old] + totals)
        chunks = [old] + [partner(old, "tiles", m) for m in masks]
    basis, dark = call(functools.partial(assemble, sz), [((r, pd), F32), ((pd // BLOCK, BLOCK), F32)], chunks)
    return basis, dark.reshape(pd), coef.T


def solution(mesh):
    return jax.shard_map(
        local,
        mesh=mesh,
        in_specs=(P("tiles", "pix"), P("tiles"), P("tiles"), P(None, "pix"), P("pix")),
        out_specs=(P(None, "pix"), P("pix"), P("tiles", None)),
        check_vma=False,
    )
```

```python
import functools

import jax
import jax.numpy as jnp
from jax import lax
from jax.experimental import pallas as pl
from jax.experimental.pallas import tpu as pltpu
from jax.sharding import PartitionSpec as P

ROW_PX = 2048
BLOCK = 128
ITERS = 2
RIDGE = 0.01
VMEM_LIMIT = 48 * 1024 * 1024

F32 = jnp.float32
BF16 = jnp.bfloat16
NN = (((1,), (0,)), ((), ()))
NT = (((1,), (1,)), ((), ()))


def params():
    return pltpu.CompilerParams(vmem_limit_bytes=VMEM_LIMIT)


def vmem(n):
    return [pl.BlockSpec(memory_space=pltpu.VMEM)] * n


SMEM = pl.BlockSpec(memory_space=pltpu.SMEM)


def split3(x):
    hi = x.astype(BF16)
    rest = x - hi.astype(F32)
    mid = rest.astype(BF16)
    low = (rest - mid.astype(F32)).astype(BF16)
    return hi, mid, low


def solve_spd(gram, sides):
    r = gram.shape[0]
    columns = [jnp.broadcast_to(gram[:, j : j + 1], (r, BLOCK)) for j in range(r)]
    rows = lax.broadcasted_iota(jnp.int32, (r, BLOCK), 0)
    for k in range(r):
        pivot = columns[k]
        inverse = 1.0 / pivot[k : k + 1, :]

        def step(x):
            scaled = x[k : k + 1, :] * inverse
            return jnp.where(rows == k, scaled, x - pivot * scaled)

        columns = columns[: k + 1] + [step(c) for c in columns[k + 1 :]]
        sides = [step(x) for x in sides]
    return sides


def eye_at(shape, first):
    row = lax.broadcasted_iota(jnp.int32, shape, 0)
    col = lax.broadcasted_iota(jnp.int32, shape, 1)
    return (col == row + first).astype(F32)


class Sizes:
    def __init__(self, tile_dev, pix_dev, rank, n_tiles, n_pix):
        self.tile_dev, self.pix_dev, self.rank = tile_dev, pix_dev, rank
        self.n_tiles, self.n_pix = n_tiles, n_pix
        self.tiles_all, self.pixels_all = tile_dev * n_tiles, pix_dev * n_pix
        self.tile_levels = levels(n_tiles)
        self.group = len(self.tile_levels[0]) + 1 if self.tile_levels else 1
        self.chunk = pix_dev // self.group
        self.blocks = self.chunk // BLOCK
        self.extra = BLOCK * (-(-2 * self.blocks // rank))
        self.stack = 6 * rank + 16
        self.spot, self.twin = rank * rank - 2, rank * rank - rank - 1


def levels(n):
    if n & (n - 1):
        return None
    out, bit = [], 1
    while bit < n:
        out.append((bit, 2 * bit, 3 * bit) if 4 * bit <= n else (bit,))
        bit *= 4
    return out


def partner(x, axis, mask):
    n = lax.axis_size(axis)
    return lax.ppermute(x, axis, [(i, i ^ mask) for i in range(n)])


def tree(parts):
    while len(parts) > 1:
        parts = [a + b for a, b in zip(parts[::2], parts[1::2])]
    return parts[0]


def sum_level(x, axis, masks):
    return tree([x] + [partner(x, axis, m) for m in masks])


def stack_block(sz, stack_ref, b, d_rows):
    r = sz.rank
    hi, mid, low = split3(b)
    for at, part in enumerate((hi, mid, low, hi, mid, hi)):
        stack_ref[at * r : (at + 1) * r, :] = part
    row = lax.broadcasted_iota(jnp.int32, (16, BLOCK), 0)
    for j, d in enumerate(d_rows):
        d_hi, d_mid, d_low = (part.astype(F32) for part in split3(d))
        tile = jnp.where(row == 0, d_hi, jnp.where(row == 1, d_mid, jnp.where(row == 2, d_low, 0.0)))
        stack_ref[6 * r : 6 * r + 16, j * BLOCK : (j + 1) * BLOCK] = tile.astype(BF16)


def project_chunk(sz, frames, stack_ref, b, d_rows, totals):
    r = sz.rank
    stack_block(sz, stack_ref, b, d_rows)
    parts = stack_ref[0 : 3 * r, :]
    proj = lax.dot_general(parts, frames, NT, preferred_element_type=F32)
    gram = lax.dot_general(parts, parts, NT, preferred_element_type=F32)
    dark = tree([b[:, j * BLOCK : (j + 1) * BLOCK] * d for j, d in enumerate(d_rows)])
    new = (proj, gram, dark)
    return new if totals is None else tuple(a + b for a, b in zip(totals, new))


def pack_projections(sz, totals, packed_ref, before_ref=None):
    r, td = sz.rank, sz.tile_dev
    proj, gram, dark = totals
    proj = proj[0:r] + proj[r : 2 * r] + proj[2 * r : 3 * r] - jnp.sum(dark, axis=1, keepdims=True)
    gram = gram[0:r] + gram[r : 2 * r] + gram[2 * r : 3 * r]
    gram = gram[:, 0:r] + gram[:, r : 2 * r] + gram[:, 2 * r : 3 * r]
    if before_ref is None:
        packed_ref[:, td : td + BLOCK] = jnp.zeros((r, BLOCK), F32)
    else:
        proj = proj + before_ref[:, 0:td]
        packed_ref[:, td : td + BLOCK] = before_ref[:, td : td + BLOCK]
        gram = gram + before_ref[:, td : td + r]
    packed_ref[:, 0:td] = proj
    packed_ref[:, td : td + r] = gram


def start_of(sz, k):
    me = lax.axis_index("tiles") & (sz.group - 1)
    return pl.multiple_of((me ^ k) * sz.chunk, BLOCK)


def first_projection(sz, f_hbm, b_hbm, d_hbm, valid_hbm, fore_hbm, f_ref, packed_ref, own_ref, least_ref, valid_ref, *refs):
    stack_refs, (b_ref, d_ref, flags_ref, sems) = refs[: sz.group], refs[sz.group :]
    small = [
        pltpu.make_async_copy(d_hbm, d_ref, sems.at[0]),
        pltpu.make_async_copy(b_hbm, b_ref, sems.at[1]),
        pltpu.make_async_copy(valid_hbm, flags_ref.at[0:1], sems.at[2]),
        pltpu.make_async_copy(fore_hbm, flags_ref.at[8:9], sems.at[3]),
    ]
    spans = [pl.ds(start_of(sz, k), sz.chunk) for k in range(sz.group)]
    large = [pltpu.make_async_copy(f_hbm.at[:, s], f_ref.at[:, s], sems.at[4 + k]) for k, s in enumerate(spans)]
    for copy in small + large:
        copy.start()
    for copy in small:
        copy.wait()
    valid = flags_ref[0:1, :] != 0
    valid_ref[...] = jnp.broadcast_to(valid.astype(F32), valid_ref.shape)
    least_ref[...] = jnp.broadcast_to(jnp.where(valid, flags_ref[8:9, :], ROW_PX), (BLOCK, sz.tile_dev)).T
    me = lax.axis_index("tiles") & (sz.group - 1)
    own_ref[:, 0 : sz.chunk] = b_ref[:, spans[0]]
    own_ref[:, sz.chunk :] = jnp.zeros((sz.rank, sz.extra), F32)
    for j in range(sz.blocks):
        own_ref[j % sz.rank, pl.ds(sz.chunk + j // sz.rank * BLOCK, BLOCK)] = d_ref[me * sz.blocks + j, :]
    totals = None
    for k in range(sz.group):
        d_rows = [d_ref[pl.ds((me ^ k) * sz.blocks + j, 1), :] for j in range(sz.blocks)]
        b = b_ref[:, spans[k]]
        large[k].wait()
        totals = project_chunk(sz, f_ref[:, spans[k]], stack_refs[k], b, d_rows, totals)
    pack_projections(sz, totals, packed_ref)


def later_projection(sz, k, f_ref, chunk_ref, *refs):
    before_ref, packed_ref, stack_ref = refs if len(refs) == 3 else (None,) + refs
    d_rows = []
    for j in range(sz.blocks):
        lane = sz.chunk + j // sz.rank * BLOCK
        d_rows.append(chunk_ref[j % sz.rank : j % sz.rank + 1, lane : lane + BLOCK])
    frames = f_ref[:, pl.ds(start_of(sz, k), sz.chunk)]
    totals = project_chunk(sz, frames, stack_ref, chunk_ref[:, 0 : sz.chunk], d_rows, None)
    pack_projections(sz, totals, packed_ref, before_ref)


def residual(sz, f_ref, stack_ref, parts, start, step, width):
    model = lax.dot_general(
        parts, stack_ref[:, step * width : (step + 1) * width], NN, preferred_element_type=F32
    )
    return f_ref[:, pl.ds(pl.multiple_of(start + step * width, BLOCK), width)].astype(F32) - model


def solve_tiles(sz, width, *refs):
    packed = refs[: sz.n_pix]
    stack_refs, refs = refs[sz.n_pix : sz.n_pix + sz.group], refs[sz.n_pix + sz.group :]
    f_ref, least_ref, valid_ref, coef_ref, three_ref, parts_ref, note_ref = refs
    r, td = sz.rank, sz.tile_dev
    a = tree([ref[...] for ref in packed]) / sz.pixels_all
    gram = a[:, td : td + r] + RIDGE * eye_at((r, r), 0)
    sides = [a[:, at : at + BLOCK] for at in range(0, td, BLOCK)]
    coef = jnp.concatenate(solve_spd(gram, sides), axis=1)
    coef_ref[...] = coef
    hi, mid, low = split3(coef)
    three_ref[...] = jnp.concatenate([hi, mid, jnp.ones((16, td), BF16), low], axis=0)
    row = lax.broadcasted_iota(jnp.int32, (BLOCK - 6 * r, td), 0)
    ones = (row < 3).astype(F32)
    hi, mid, low = hi.astype(F32), mid.astype(F32), low.astype(F32)
    parts = jnp.concatenate([hi, hi, hi, mid, mid, low, ones], axis=0).T.astype(BF16)
    parts_ref[...] = parts
    parts = parts[:, 0 : sz.stack]
    least = least_ref[...]

    total = jnp.zeros((8, BLOCK), F32)
    for k, stack_ref in enumerate(stack_refs):
        start = start_of(sz, k)
        for step in range(sz.chunk // width):
            res = residual(sz, f_ref, stack_ref, parts, start, step, width)
            square = res * res
            for j in range(width // BLOCK):
                block = (start // BLOCK + step * (width // BLOCK) + j) % (ROW_PX // BLOCK)
                term = jnp.where(least <= block, square[:, j * BLOCK : (j + 1) * BLOCK], 0.0)
                total = total + jnp.sum(term.reshape(td // 8, 8, BLOCK), axis=0)
    total = jnp.sum(jnp.sum(total, axis=0, keepdims=True), axis=1, keepdims=True)
    products = jnp.concatenate([coef[i : i + 1] * coef for i in range(r)], axis=0)
    ones = valid_ref[...].astype(BF16)
    flat = sum(lax.dot_general(ones, part, NT, preferred_element_type=F32) for part in split3(products))
    lane = lax.broadcasted_iota(jnp.int32, flat.shape, 1)
    flat = jnp.where(lane == sz.spot, total, flat)
    for at in range(0, note_ref.shape[0], 8):
        note_ref[at : at + 8, :] = flat


def invert_gram(sz, note_ref, inverse_ref):
    r = sz.rank
    flat = jnp.sum(note_ref[...], axis=0, keepdims=True)
    gram = jnp.concatenate([flat[:, i * r : (i + 1) * r] for i in range(r)], axis=0)
    row = lax.broadcasted_iota(jnp.int32, (r, r), 0)
    col = lax.broadcasted_iota(jnp.int32, (r, r), 1)
    twin = flat[:, sz.twin : sz.twin + 1]
    gram = jnp.where((row == r - 1) & (col == r - 2), twin, gram)
    gram = gram / (sz.n_pix * sz.tiles_all) + RIDGE * eye_at((r, r), 0)
    (inverse_ref[...],) = solve_spd(gram, [eye_at((r, BLOCK), 0)])


def update_terms(sz, width, k, note_ref, f_ref, stack_ref, least_ref, three_ref, parts_ref, out_ref):
    r = sz.rank
    start = start_of(sz, k)
    total = jnp.sum(note_ref[:, sz.spot : sz.spot + 1], axis=0, keepdims=True)
    spread = total / (sz.tiles_all * sz.pixels_all) + 1e-05
    scale = jnp.broadcast_to(1.0 / (4.0 * spread), (8, BLOCK))[0:1, :]
    parts = parts_ref[:, 0 : sz.stack]
    three = three_ref[...]
    two = three[0 : 2 * r + 16]
    least = least_ref[...]
    each = width // BLOCK

    def place(flat):
        lane = sz.chunk + flat // r * BLOCK
        return slice(flat % r, flat % r + 1), slice(lane, lane + BLOCK)

    for step in range(sz.chunk // width):
        res = residual(sz, f_ref, stack_ref, parts, start, step, width)
        hi_parts, mid_parts = [], []
        for j in range(each):
            block = (start // BLOCK + step * each + j) % (ROW_PX // BLOCK)
            x = res[:, j * BLOCK : (j + 1) * BLOCK]
            g = jnp.where(least <= block, pl.reciprocal(x * x * scale + 1.0, approx=True), 0.0)
            out_ref[place(sz.blocks + step * each + j)] = jnp.sum(g, axis=0, keepdims=True)
            w = g * x
            w_hi = w.astype(BF16)
            hi_parts.append(w_hi)
            mid_parts.append((w - w_hi.astype(F32)).astype(BF16))
        terms = lax.dot_general(three, jnp.concatenate(hi_parts, axis=1), NN, preferred_element_type=F32)
        more = lax.dot_general(two, jnp.concatenate(mid_parts, axis=1), NN, preferred_element_type=F32)
        out_ref[:, step * width : (step + 1) * width] = terms[0:r] + (
            terms[r : 2 * r] + terms[2 * r + 16 :] + more[0:r] + more[r : 2 * r]
        )
        sums = terms[2 * r : 2 * r + 1] + more[2 * r : 2 * r + 1]
        for j in range(each):
            out_ref[place(step * each + j)] = sums[:, j * BLOCK : (j + 1) * BLOCK]
    used = 2 * sz.blocks
    if used % r:
        out_ref[used % r :, sz.chunk + used // r * BLOCK :] = jnp.zeros((r - used % r, BLOCK), F32)


def update_chunk(sz, inverse_ref, old_ref, *refs):
    total_refs, new_ref = refs[:-1], refs[-1]
    r = sz.rank
    totals = tree([ref[...] for ref in total_refs])
    inverse = inverse_ref[:, 0:r]
    change = jnp.dot(inverse, totals[:, 0 : sz.chunk] / sz.tiles_all, precision=lax.Precision.HIGHEST, preferred_element_type=F32)
    new_ref[:, 0 : sz.chunk] = old_ref[:, 0 : sz.chunk] + change
    new_ref[:, sz.chunk :] = jnp.zeros((r, sz.extra), F32)

    def place(flat):
        return flat % r, sz.chunk + flat // r * BLOCK

    many = 8 if sz.blocks % 8 == 0 else 1
    for j in range(0, sz.blocks, many):
        (row, lane), (row_g, lane_g) = place(j), place(sz.blocks + j)
        w = totals[row : row + many, lane : lane + BLOCK]
        g = totals[row_g : row_g + many, lane_g : lane_g + BLOCK]
        new_ref[row : row + many, lane : lane + BLOCK] = (
            old_ref[row : row + many, lane : lane + BLOCK] + w / (g + 1.0)
        )


def assemble(sz, coef_ref, *refs):
    chunks, (b_ref, d_ref, coef_out_ref) = refs[: sz.group], refs[sz.group :]
    coef_out_ref[...] = coef_ref[...]
    me = lax.axis_index("tiles") & (sz.group - 1)
    for k, ref in enumerate(chunks):
        c = me ^ k
        b_ref[:, pl.ds(pl.multiple_of(c * sz.chunk, BLOCK), sz.chunk)] = ref[:, 0 : sz.chunk]
        for j in range(sz.blocks):
            lane = sz.chunk + j // sz.rank * BLOCK
            d_ref[c * sz.blocks + j, :] = ref[j % sz.rank, lane : lane + BLOCK]


def call(body, outs, ins, in_hbm=False, scratch=()):
    return pl.pallas_call(
        body,
        out_shape=[jax.ShapeDtypeStruct(s, t) for s, t in outs],
        in_specs=[pl.BlockSpec(memory_space=pltpu.HBM)] * len(ins) if in_hbm else vmem(len(ins)),
        out_specs=vmem(len(outs)),
        scratch_shapes=scratch,
        compiler_params=params(),
    )(*([pltpu.with_memory_space_constraint(x, pltpu.HBM) for x in ins] if in_hbm else ins))


def local(frames, tile_valid, foreground_blocks, basis_start, dark_start):
    td, pd = frames.shape
    r = basis_start.shape[0]
    sz = Sizes(td, pd, r, lax.axis_size("tiles"), lax.axis_size("pix"))
    everyone = ("tiles", "pix")
    devices = sz.n_tiles * sz.n_pix
    pix_masks = range(1, sz.n_pix)
    width = min(256, sz.chunk)
    chunk_shape = (r, sz.chunk + sz.extra)
    packed_out = ((r, td + BLOCK), F32)
    stack_out = ((sz.stack, sz.chunk), BF16)
    masks = sz.tile_levels[0]
    for iteration in range(ITERS):
        if iteration == 0:
            frames, packed, old, least, valid, *stacks = call(
                functools.partial(first_projection, sz),
                [((td, pd), BF16), packed_out, (chunk_shape, F32), ((td, BLOCK), jnp.int32), ((8, td), F32)]
                + [stack_out] * sz.group,
                [frames, basis_start, dark_start.reshape(pd // BLOCK, BLOCK), tile_valid.reshape(1, td), foreground_blocks.reshape(1, td)],
                in_hbm=True,
                scratch=[
                    pltpu.VMEM((r, pd), F32),
                    pltpu.VMEM((pd // BLOCK, BLOCK), F32),
                    pltpu.VMEM((16, td), jnp.int32),
                    pltpu.SemaphoreType.DMA((4 + sz.group,)),
                ],
            )
        else:
            before, stacks = [], [None] * sz.group
            for k in [0] + list(masks)[::-1]:
                packed, stacks[k] = call(
                    functools.partial(later_projection, sz, k), [packed_out, stack_out], [frames, chunks[k]] + before
                )
                before = [packed]
        both = [packed] + [partner(packed, "pix", m) for m in pix_masks]
        coef, three, parts, note = call(
            functools.partial(solve_tiles, sz, width),
            [((r, td), F32), ((3 * r + 16, td), BF16), ((td, BLOCK), BF16), ((devices, r * r), F32)],
            both + stacks + [frames, least, valid],
        )
        notes = lax.all_to_all(note, everyone, 0, 0, tiled=True)
        (inverse,) = call(functools.partial(invert_gram, sz), [((r, BLOCK), F32)], [notes])
        terms = {}
        for k in list(masks) + [0]:
            (terms[k],) = call(
                functools.partial(update_terms, sz, width, k),
                [(chunk_shape, F32)],
                [notes, frames, stacks[k], least, three, parts],
            )
        total = tree([terms[0]] + [partner(terms[m], "tiles", m) for m in masks])
        later = sz.tile_levels[1:]
        for level in later[:-1]:
            total = sum_level(total, "tiles", level)
        totals = [total] + [partner(total, "tiles", m) for m in (later[-1] if later else ())]
        (old,) = call(functools.partial(update_chunk, sz), [(chunk_shape, F32)], [inverse, old] + totals)
        chunks = [old] + [partner(old, "tiles", m) for m in masks]
    basis, dark, coef = call(
        functools.partial(assemble, sz),
        [((r, pd), F32), ((pd // BLOCK, BLOCK), F32), ((r, td), F32)],
        [coef] + chunks,
    )
    return basis, dark.reshape(pd), coef.T


def solution(mesh):
    return jax.shard_map(
        local,
        mesh=mesh,
        in_specs=(P("tiles", "pix"), P("tiles"), P("tiles"), P(None, "pix"), P("pix")),
        out_specs=(P(None, "pix"), P("pix"), P("tiles", None)),
        check_vma=False,
    )
```

```python
import functools

import jax
import jax.numpy as jnp
from jax import lax
from jax.experimental import pallas as pl
from jax.experimental.pallas import tpu as pltpu
from jax.sharding import PartitionSpec as P

ROW_PX = 2048
BLOCK = 128
ITERS = 2
RIDGE = 0.01
VMEM_LIMIT = 48 * 1024 * 1024

F32 = jnp.float32
BF16 = jnp.bfloat16
NN = (((1,), (0,)), ((), ()))
NT = (((1,), (1,)), ((), ()))


def params():
    return pltpu.CompilerParams(vmem_limit_bytes=VMEM_LIMIT)


def vmem(n):
    return [pl.BlockSpec(memory_space=pltpu.VMEM)] * n


SMEM = pl.BlockSpec(memory_space=pltpu.SMEM)


def split3(x):
    hi = x.astype(BF16)
    rest = x - hi.astype(F32)
    mid = rest.astype(BF16)
    low = (rest - mid.astype(F32)).astype(BF16)
    return hi, mid, low


def solve_spd(gram, sides):
    r = gram.shape[0]
    columns = [jnp.broadcast_to(gram[:, j : j + 1], (r, BLOCK)) for j in range(r)]
    rows = lax.broadcasted_iota(jnp.int32, (r, BLOCK), 0)
    for k in range(r):
        pivot = columns[k]
        inverse = 1.0 / pivot[k : k + 1, :]

        def step(x):
            scaled = x[k : k + 1, :] * inverse
            return jnp.where(rows == k, scaled, x - pivot * scaled)

        columns = columns[: k + 1] + [step(c) for c in columns[k + 1 :]]
        sides = [step(x) for x in sides]
    return sides


def eye_at(shape, first):
    row = lax.broadcasted_iota(jnp.int32, shape, 0)
    col = lax.broadcasted_iota(jnp.int32, shape, 1)
    return (col == row + first).astype(F32)


ORDER = ((0, 1, 2), (2, 1, 0), (2, 1, 0), (2, 1, 0))


def permuted(masks, order):
    return [masks[i] for i in order] if len(masks) == 3 else list(masks)


class Sizes:
    def __init__(self, tile_dev, pix_dev, rank, n_tiles, n_pix):
        self.tile_dev, self.pix_dev, self.rank = tile_dev, pix_dev, rank
        self.n_tiles, self.n_pix = n_tiles, n_pix
        self.tiles_all, self.pixels_all = tile_dev * n_tiles, pix_dev * n_pix
        self.tile_levels = levels(n_tiles)
        self.group = len(self.tile_levels[0]) + 1 if self.tile_levels else 1
        self.chunk = pix_dev // self.group
        self.blocks = self.chunk // BLOCK
        self.extra = BLOCK * (-(-2 * self.blocks // rank))
        self.stack = 6 * rank + 16
        self.spot, self.twin = rank * rank - 2, rank * rank - rank - 1


def levels(n):
    if n & (n - 1):
        return None
    out, bit = [], 1
    while bit < n:
        out.append((bit, 2 * bit, 3 * bit) if 4 * bit <= n else (bit,))
        bit *= 4
    return out


def partner(x, axis, mask):
    n = lax.axis_size(axis)
    return lax.ppermute(x, axis, [(i, i ^ mask) for i in range(n)])


def tree(parts):
    while len(parts) > 1:
        parts = [a + b for a, b in zip(parts[::2], parts[1::2])]
    return parts[0]


def sum_level(x, axis, masks):
    return tree([x] + [partner(x, axis, m) for m in masks])


def stack_block(sz, stack_ref, b, d_rows):
    r = sz.rank
    hi, mid, low = split3(b)
    for at, part in enumerate((hi, mid, low, hi, mid, hi)):
        stack_ref[at * r : (at + 1) * r, :] = part
    row = lax.broadcasted_iota(jnp.int32, (16, BLOCK), 0)
    for j, d in enumerate(d_rows):
        d_hi, d_mid, d_low = (part.astype(F32) for part in split3(d))
        tile = jnp.where(row == 0, d_hi, jnp.where(row == 1, d_mid, jnp.where(row == 2, d_low, 0.0)))
        stack_ref[6 * r : 6 * r + 16, j * BLOCK : (j + 1) * BLOCK] = tile.astype(BF16)


def project_chunk(sz, frames, stack_ref, b, d_rows, totals):
    r = sz.rank
    stack_block(sz, stack_ref, b, d_rows)
    parts = stack_ref[0 : 3 * r, :]
    proj = lax.dot_general(parts, frames, NT, preferred_element_type=F32)
    gram = lax.dot_general(parts, parts, NT, preferred_element_type=F32)
    dark = tree([b[:, j * BLOCK : (j + 1) * BLOCK] * d for j, d in enumerate(d_rows)])
    new = (proj, gram, dark)
    return new if totals is None else tuple(a + b for a, b in zip(totals, new))


def pack_projections(sz, totals, packed_ref, before_ref=None):
    r, td = sz.rank, sz.tile_dev
    proj, gram, dark = totals
    proj = proj[0:r] + proj[r : 2 * r] + proj[2 * r : 3 * r] - jnp.sum(dark, axis=1, keepdims=True)
    gram = gram[0:r] + gram[r : 2 * r] + gram[2 * r : 3 * r]
    gram = gram[:, 0:r] + gram[:, r : 2 * r] + gram[:, 2 * r : 3 * r]
    if before_ref is None:
        packed_ref[:, td : td + BLOCK] = jnp.zeros((r, BLOCK), F32)
    else:
        proj = proj + before_ref[:, 0:td]
        packed_ref[:, td : td + BLOCK] = before_ref[:, td : td + BLOCK]
        gram = gram + before_ref[:, td : td + r]
    packed_ref[:, 0:td] = proj
    packed_ref[:, td : td + r] = gram


def start_of(sz, k):
    me = lax.axis_index("tiles") & (sz.group - 1)
    return pl.multiple_of((me ^ k) * sz.chunk, BLOCK)


def first_projection(sz, f_hbm, b_hbm, d_hbm, valid_hbm, fore_hbm, f_ref, packed_ref, own_ref, least_ref, bar_ref, valid_ref, *refs):
    stack_refs, (b_ref, d_ref, flags_ref, sems) = refs[: sz.group], refs[sz.group :]
    small = [
        pltpu.make_async_copy(d_hbm, d_ref, sems.at[0]),
        pltpu.make_async_copy(b_hbm, b_ref, sems.at[1]),
        pltpu.make_async_copy(valid_hbm, flags_ref.at[0:1], sems.at[2]),
        pltpu.make_async_copy(fore_hbm, flags_ref.at[8:9], sems.at[3]),
    ]
    spans = [pl.ds(start_of(sz, k), sz.chunk) for k in range(sz.group)]
    large = [pltpu.make_async_copy(f_hbm.at[:, s], f_ref.at[:, s], sems.at[4 + k]) for k, s in enumerate(spans)]
    for copy in small + large:
        copy.start()
    for copy in small[:2]:
        copy.wait()
    me = lax.axis_index("tiles") & (sz.group - 1)
    own_ref[:, 0 : sz.chunk] = b_ref[:, spans[0]]
    own_ref[:, sz.chunk :] = jnp.zeros((sz.rank, sz.extra), F32)
    for j in range(sz.blocks):
        own_ref[j % sz.rank, pl.ds(sz.chunk + j // sz.rank * BLOCK, BLOCK)] = d_ref[me * sz.blocks + j, :]
    bases = [b_ref[:, span] for span in spans]
    darks = [[d_ref[pl.ds((me ^ k) * sz.blocks + j, 1), :] for j in range(sz.blocks)] for k in range(sz.group)]
    for k in range(sz.group):
        stack_block(sz, stack_refs[k], bases[k], darks[k])
    parts = [ref[0 : 3 * sz.rank, :] for ref in stack_refs]
    gram = tree([lax.dot_general(p, p, NT, preferred_element_type=F32) for p in parts])
    dark = tree([b[:, j * BLOCK : (j + 1) * BLOCK] * d for b, rows in zip(bases, darks) for j, d in enumerate(rows)])
    for copy in small[2:]:
        copy.wait()
    valid = flags_ref[0:1, :] != 0
    valid_ref[...] = jnp.broadcast_to(valid.astype(F32), valid_ref.shape)
    least = jnp.broadcast_to(jnp.where(valid, flags_ref[8:9, :], ROW_PX), (BLOCK, sz.tile_dev)).T
    least_ref[...] = least
    for block in range(bar_ref.shape[0]):
        bar_ref[block] = jnp.where(least <= block, 1.0, jnp.inf)
    for copy in large:
        copy.wait()
    proj = tree([lax.dot_general(p, f_ref[:, s], NT, preferred_element_type=F32) for p, s in zip(parts, spans)])
    pack_projections(sz, (proj, gram, dark), packed_ref)


def later_projection(sz, k, f_ref, chunk_ref, *refs):
    before_ref, packed_ref, stack_ref = refs if len(refs) == 3 else (None,) + refs
    d_rows = []
    for j in range(sz.blocks):
        lane = sz.chunk + j // sz.rank * BLOCK
        d_rows.append(chunk_ref[j % sz.rank : j % sz.rank + 1, lane : lane + BLOCK])
    frames = f_ref[:, pl.ds(start_of(sz, k), sz.chunk)]
    totals = project_chunk(sz, frames, stack_ref, chunk_ref[:, 0 : sz.chunk], d_rows, None)
    pack_projections(sz, totals, packed_ref, before_ref)


def residual(sz, f_ref, stack_ref, parts, start, step, width):
    model = lax.dot_general(
        parts, stack_ref[:, step * width : (step + 1) * width], NN, preferred_element_type=F32
    )
    return f_ref[:, pl.ds(pl.multiple_of(start + step * width, BLOCK), width)].astype(F32) - model


def solve_tiles(sz, width, *refs):
    packed = refs[: sz.n_pix]
    stack_refs, refs = refs[sz.n_pix : sz.n_pix + sz.group], refs[sz.n_pix + sz.group :]
    f_ref, least_ref, valid_ref, coef_ref, three_ref, parts_ref, note_ref = refs
    r, td = sz.rank, sz.tile_dev
    a = tree([ref[...] for ref in packed]) / sz.pixels_all
    gram = a[:, td : td + r] + RIDGE * eye_at((r, r), 0)
    sides = [a[:, at : at + BLOCK] for at in range(0, td, BLOCK)]
    coef = jnp.concatenate(solve_spd(gram, sides), axis=1)
    coef_ref[...] = coef
    hi, mid, low = split3(coef)
    three_ref[...] = jnp.concatenate([hi, mid, jnp.ones((16, td), BF16), low], axis=0)
    row = lax.broadcasted_iota(jnp.int32, (BLOCK - 6 * r, td), 0)
    ones = (row < 3).astype(F32)
    hi, mid, low = hi.astype(F32), mid.astype(F32), low.astype(F32)
    parts = jnp.concatenate([hi, hi, hi, mid, mid, low, ones], axis=0).T.astype(BF16)
    parts_ref[...] = parts
    parts = parts[:, 0 : sz.stack]
    least = least_ref[...]

    total = jnp.zeros((8, BLOCK), F32)
    for k, stack_ref in enumerate(stack_refs):
        start = start_of(sz, k)
        for step in range(sz.chunk // width):
            res = residual(sz, f_ref, stack_ref, parts, start, step, width)
            square = res * res
            for j in range(width // BLOCK):
                block = (start // BLOCK + step * (width // BLOCK) + j) % (ROW_PX // BLOCK)
                term = jnp.where(least <= block, square[:, j * BLOCK : (j + 1) * BLOCK], 0.0)
                total = total + jnp.sum(term.reshape(td // 8, 8, BLOCK), axis=0)
    total = jnp.sum(jnp.sum(total, axis=0, keepdims=True), axis=1, keepdims=True)
    products = jnp.concatenate([coef[i : i + 1] * coef for i in range(r)], axis=0)
    ones = valid_ref[...].astype(BF16)
    flat = sum(lax.dot_general(ones, part, NT, preferred_element_type=F32) for part in split3(products))
    lane = lax.broadcasted_iota(jnp.int32, flat.shape, 1)
    flat = jnp.where(lane == sz.spot, total, flat)
    for at in range(0, note_ref.shape[0], 8):
        note_ref[at : at + 8, :] = flat


def invert_gram(sz, note_ref, inverse_ref):
    r = sz.rank
    flat = jnp.sum(note_ref[...], axis=0, keepdims=True)
    gram = jnp.concatenate([flat[:, i * r : (i + 1) * r] for i in range(r)], axis=0)
    row = lax.broadcasted_iota(jnp.int32, (r, r), 0)
    col = lax.broadcasted_iota(jnp.int32, (r, r), 1)
    twin = flat[:, sz.twin : sz.twin + 1]
    gram = jnp.where((row == r - 1) & (col == r - 2), twin, gram)
    gram = gram / (sz.n_pix * sz.tiles_all) + RIDGE * eye_at((r, r), 0)
    (inverse_ref[...],) = solve_spd(gram, [eye_at((r, BLOCK), 0)])


def update_terms(sz, width, ks, note_ref, f_ref, bar_ref, three_ref, parts_ref, *refs):
    r = sz.rank
    total = jnp.sum(note_ref[:, sz.spot : sz.spot + 1], axis=0, keepdims=True)
    spread = total / (sz.tiles_all * sz.pixels_all) + 1e-05
    scale = jnp.broadcast_to(1.0 / (4.0 * spread), (8, BLOCK))[0:1, :]
    for k, stack_ref, out_ref in zip(ks, refs[: len(ks)], refs[len(ks) :]):
        chunk_terms(sz, width, k, scale, f_ref, stack_ref, bar_ref, three_ref, parts_ref, out_ref)


def chunk_terms(sz, width, k, scale, f_ref, stack_ref, bar_ref, three_ref, parts_ref, out_ref):
    r = sz.rank
    start = start_of(sz, k)
    parts = parts_ref[:, 0 : sz.stack]
    three = three_ref[...]
    two = three[0 : 2 * r + 16]
    each = width // BLOCK

    def place(flat):
        lane = sz.chunk + flat // r * BLOCK
        return slice(flat % r, flat % r + 1), slice(lane, lane + BLOCK)

    for step in range(sz.chunk // width):
        res = residual(sz, f_ref, stack_ref, parts, start, step, width)
        hi_parts, mid_parts = [], []
        for j in range(each):
            block = (start // BLOCK + step * each + j) % (ROW_PX // BLOCK)
            x = res[:, j * BLOCK : (j + 1) * BLOCK]
            g = pl.reciprocal(x * x * scale + bar_ref[jnp.minimum(block, bar_ref.shape[0] - 1)], approx=True)
            out_ref[place(sz.blocks + step * each + j)] = jnp.sum(g, axis=0, keepdims=True)
            w = g * x
            w_hi = w.astype(BF16)
            hi_parts.append(w_hi)
            mid_parts.append((w - w_hi.astype(F32)).astype(BF16))
        terms = lax.dot_general(three, jnp.concatenate(hi_parts, axis=1), NN, preferred_element_type=F32)
        more = lax.dot_general(two, jnp.concatenate(mid_parts, axis=1), NN, preferred_element_type=F32)
        out_ref[:, step * width : (step + 1) * width] = terms[0:r] + (
            terms[r : 2 * r] + terms[2 * r + 16 :] + more[0:r] + more[r : 2 * r]
        )
        sums = terms[2 * r : 2 * r + 1] + more[2 * r : 2 * r + 1]
        for j in range(each):
            out_ref[place(step * each + j)] = sums[:, j * BLOCK : (j + 1) * BLOCK]
    used = 2 * sz.blocks
    if used % r:
        out_ref[used % r :, sz.chunk + used // r * BLOCK :] = jnp.zeros((r - used % r, BLOCK), F32)


def update_chunk(sz, places, inverse_ref, old_ref, *refs):
    total_refs, new_ref = refs[:-1], refs[-1]
    r = sz.rank
    totals = tree([total_refs[i][...] for i in places])
    inverse = inverse_ref[:, 0:r]
    change = jnp.dot(inverse, totals[:, 0 : sz.chunk] / sz.tiles_all, precision=lax.Precision.HIGHEST, preferred_element_type=F32)
    new_ref[:, 0 : sz.chunk] = old_ref[:, 0 : sz.chunk] + change
    new_ref[:, sz.chunk :] = jnp.zeros((r, sz.extra), F32)

    def place(flat):
        return flat % r, sz.chunk + flat // r * BLOCK

    many = 8 if sz.blocks % 8 == 0 else 1
    for j in range(0, sz.blocks, many):
        (row, lane), (row_g, lane_g) = place(j), place(sz.blocks + j)
        w = totals[row : row + many, lane : lane + BLOCK]
        g = totals[row_g : row_g + many, lane_g : lane_g + BLOCK]
        new_ref[row : row + many, lane : lane + BLOCK] = (
            old_ref[row : row + many, lane : lane + BLOCK] + w / (g + 1.0)
        )


def assemble(sz, ks, coef_ref, *refs):
    chunks, (b_ref, d_ref, coef_out_ref) = refs[: sz.group], refs[sz.group :]
    coef_out_ref[...] = coef_ref[...]
    me = lax.axis_index("tiles") & (sz.group - 1)
    for k, ref in zip(ks, chunks):
        c = me ^ k
        b_ref[:, pl.ds(pl.multiple_of(c * sz.chunk, BLOCK), sz.chunk)] = ref[:, 0 : sz.chunk]
        for j in range(sz.blocks):
            lane = sz.chunk + j // sz.rank * BLOCK
            d_ref[c * sz.blocks + j, :] = ref[j % sz.rank, lane : lane + BLOCK]


def call(body, outs, ins, in_hbm=False, scratch=()):
    return pl.pallas_call(
        body,
        out_shape=[jax.ShapeDtypeStruct(s, t) for s, t in outs],
        in_specs=[pl.BlockSpec(memory_space=pltpu.HBM)] * len(ins) if in_hbm else vmem(len(ins)),
        out_specs=vmem(len(outs)),
        scratch_shapes=scratch,
        compiler_params=params(),
    )(*([pltpu.with_memory_space_constraint(x, pltpu.HBM) for x in ins] if in_hbm else ins))


def local(frames, tile_valid, foreground_blocks, basis_start, dark_start):
    td, pd = frames.shape
    r = basis_start.shape[0]
    sz = Sizes(td, pd, r, lax.axis_size("tiles"), lax.axis_size("pix"))
    everyone = ("tiles", "pix")
    devices = sz.n_tiles * sz.n_pix
    pix_masks = range(1, sz.n_pix)
    width = min(256, sz.chunk)
    chunk_shape = (r, sz.chunk + sz.extra)
    packed_out = ((r, td + BLOCK), F32)
    stack_out = ((sz.stack, sz.chunk), BF16)
    masks = sz.tile_levels[0]
    for iteration in range(ITERS):
        if iteration == 0:
            frames, packed, old, least, bar, valid, *stacks = call(
                functools.partial(first_projection, sz),
                [((td, pd), BF16), packed_out, (chunk_shape, F32), ((td, BLOCK), jnp.int32), ((ROW_PX // BLOCK // 2 + 1, td, BLOCK), F32), ((8, td), F32)]
                + [stack_out] * sz.group,
                [frames, basis_start, dark_start.reshape(pd // BLOCK, BLOCK), tile_valid.reshape(1, td), foreground_blocks.reshape(1, td)],
                in_hbm=True,
                scratch=[
                    pltpu.VMEM((r, pd), F32),
                    pltpu.VMEM((pd // BLOCK, BLOCK), F32),
                    pltpu.VMEM((16, td), jnp.int32),
                    pltpu.SemaphoreType.DMA((4 + sz.group,)),
                ],
            )
        else:
            before, stacks = [], [None] * sz.group
            for k in [0] + permuted(masks, ORDER[2]):
                packed, stacks[k] = call(
                    functools.partial(later_projection, sz, k), [packed_out, stack_out], [frames, chunks[k]] + before
                )
                before = [packed]
        both = [packed] + [partner(packed, "pix", m) for m in pix_masks]
        coef, three, parts, note = call(
            functools.partial(solve_tiles, sz, width),
            [((r, td), F32), ((3 * r + 16, td), BF16), ((td, BLOCK), BF16), ((devices, r * r), F32)],
            both + stacks + [frames, least, valid],
        )
        notes = lax.all_to_all(note, everyone, 0, 0, tiled=True)
        (inverse,) = call(functools.partial(invert_gram, sz), [((r, BLOCK), F32)], [notes])
        terms = {}
        for ks in (list(masks), [0]):
            outs = call(
                functools.partial(update_terms, sz, width, ks),
                [(chunk_shape, F32)] * len(ks),
                [notes, frames, bar, three, parts] + [stacks[k] for k in ks],
            )
            terms.update(zip(ks, outs))
        order = permuted(masks, ORDER[0])
        got = dict(zip(order, lax.optimization_barrier([partner(terms[m], "tiles", m) for m in order])))
        total = tree([terms[0]] + [got[m] for m in masks])
        later = sz.tile_levels[1:]
        for level in later[:-1]:
            total = sum_level(total, "tiles", level)
        last = later[-1] if later else ()
        order = permuted(last, ORDER[1])
        totals = [total] + [partner(total, "tiles", m) for m in order]
        places = [0] + [1 + order.index(m) for m in last]
        (old,) = call(functools.partial(update_chunk, sz, places), [(chunk_shape, F32)], [inverse, old] + totals)
        chunks = [old] + [partner(old, "tiles", m) for m in masks]
    ks = [0] + permuted(masks, ORDER[3])
    basis, dark, coef = call(
        functools.partial(assemble, sz, ks),
        [((r, pd), F32), ((pd // BLOCK, BLOCK), F32), ((r, td), F32)],
        [coef] + [chunks[k] for k in ks],
    )
    return basis, dark.reshape(pd), coef.T


def solution(mesh):
    return jax.shard_map(
        local,
        mesh=mesh,
        in_specs=(P("tiles", "pix"), P("tiles"), P("tiles"), P(None, "pix"), P("pix")),
        out_specs=(P(None, "pix"), P("pix"), P("tiles", None)),
        check_vma=False,
    )
```

```python
import functools

import jax
import jax.numpy as jnp
from jax import lax
from jax.experimental import pallas as pl
from jax.experimental.pallas import tpu as pltpu
from jax.sharding import PartitionSpec as P

ROW_PX = 2048
BLOCK = 128
ITERS = 2
RIDGE = 0.01
VMEM_LIMIT = 48 * 1024 * 1024

F32 = jnp.float32
BF16 = jnp.bfloat16
NN = (((1,), (0,)), ((), ()))
NT = (((1,), (1,)), ((), ()))


def params():
    return pltpu.CompilerParams(vmem_limit_bytes=VMEM_LIMIT)


def vmem(n):
    return [pl.BlockSpec(memory_space=pltpu.VMEM)] * n


SMEM = pl.BlockSpec(memory_space=pltpu.SMEM)


def split3(x):
    hi = x.astype(BF16)
    rest = x - hi.astype(F32)
    mid = rest.astype(BF16)
    low = (rest - mid.astype(F32)).astype(BF16)
    return hi, mid, low


def solve_spd(gram, sides):
    r = gram.shape[0]
    columns = [jnp.broadcast_to(gram[:, j : j + 1], (r, BLOCK)) for j in range(r)]
    rows = lax.broadcasted_iota(jnp.int32, (r, BLOCK), 0)
    for k in range(r):
        pivot = columns[k]
        inverse = 1.0 / pivot[k : k + 1, :]

        def step(x):
            scaled = x[k : k + 1, :] * inverse
            return jnp.where(rows == k, scaled, x - pivot * scaled)

        columns = columns[: k + 1] + [step(c) for c in columns[k + 1 :]]
        sides = [step(x) for x in sides]
    return sides


def eye_at(shape, first):
    row = lax.broadcasted_iota(jnp.int32, shape, 0)
    col = lax.broadcasted_iota(jnp.int32, shape, 1)
    return (col == row + first).astype(F32)


ORDER = ((0, 1, 2), (2, 0, 1), (2, 1, 0), (2, 1, 0))


def permuted(masks, order):
    return [masks[i] for i in order] if len(masks) == 3 else list(masks)


class Sizes:
    def __init__(self, tile_dev, pix_dev, rank, n_tiles, n_pix):
        self.tile_dev, self.pix_dev, self.rank = tile_dev, pix_dev, rank
        self.n_tiles, self.n_pix = n_tiles, n_pix
        self.tiles_all, self.pixels_all = tile_dev * n_tiles, pix_dev * n_pix
        self.tile_levels = levels(n_tiles)
        self.group = len(self.tile_levels[0]) + 1 if self.tile_levels else 1
        self.chunk = pix_dev // self.group
        self.blocks = self.chunk // BLOCK
        self.extra = BLOCK * (-(-2 * self.blocks // rank))
        self.stack = 6 * rank + 16
        self.spot, self.twin = rank * rank - 2, rank * rank - rank - 1


def levels(n):
    if n & (n - 1):
        return None
    out, bit = [], 1
    while bit < n:
        out.append((bit, 2 * bit, 3 * bit) if 4 * bit <= n else (bit,))
        bit *= 4
    return out


def partner(x, axis, mask):
    n = lax.axis_size(axis)
    return lax.ppermute(x, axis, [(i, i ^ mask) for i in range(n)])


def crossed(x, mask, swap):
    n, cores = lax.axis_size("tiles"), lax.axis_size("pix")
    pairs = []
    for i in range(n):
        for p in range(cores):
            pairs.append((i * cores + p, (i ^ (swap.get(mask, mask) if p & 1 else mask)) * cores + p))
    return lax.ppermute(x, ("tiles", "pix"), pairs)


def tree(parts):
    while len(parts) > 1:
        parts = [a + b for a, b in zip(parts[::2], parts[1::2])]
    return parts[0]


def sum_level(x, axis, masks):
    return tree([x] + [partner(x, axis, m) for m in masks])


def stack_block(sz, stack_ref, b, d_rows):
    r = sz.rank
    hi, mid, low = split3(b)
    for at, part in enumerate((hi, mid, low, hi, mid, hi)):
        stack_ref[at * r : (at + 1) * r, :] = part
    row = lax.broadcasted_iota(jnp.int32, (16, BLOCK), 0)
    for j, d in enumerate(d_rows):
        d_hi, d_mid, d_low = (part.astype(F32) for part in split3(d))
        tile = jnp.where(row == 0, d_hi, jnp.where(row == 1, d_mid, jnp.where(row == 2, d_low, 0.0)))
        stack_ref[6 * r : 6 * r + 16, j * BLOCK : (j + 1) * BLOCK] = tile.astype(BF16)


def project_chunk(sz, frames, stack_ref, b, d_rows, totals):
    r = sz.rank
    stack_block(sz, stack_ref, b, d_rows)
    parts = stack_ref[0 : 3 * r, :]
    proj = lax.dot_general(parts, frames, NT, preferred_element_type=F32)
    gram = lax.dot_general(parts, parts, NT, preferred_element_type=F32)
    dark = tree([b[:, j * BLOCK : (j + 1) * BLOCK] * d for j, d in enumerate(d_rows)])
    new = (proj, gram, dark)
    return new if totals is None else tuple(a + b for a, b in zip(totals, new))


def pack_projections(sz, totals, packed_ref, before_ref=None):
    r, td = sz.rank, sz.tile_dev
    proj, gram, dark = totals
    proj = proj[0:r] + proj[r : 2 * r] + proj[2 * r : 3 * r] - jnp.sum(dark, axis=1, keepdims=True)
    gram = gram[0:r] + gram[r : 2 * r] + gram[2 * r : 3 * r]
    gram = gram[:, 0:r] + gram[:, r : 2 * r] + gram[:, 2 * r : 3 * r]
    if before_ref is None:
        packed_ref[:, td : td + BLOCK] = jnp.zeros((r, BLOCK), F32)
    else:
        proj = proj + before_ref[:, 0:td]
        packed_ref[:, td : td + BLOCK] = before_ref[:, td : td + BLOCK]
        gram = gram + before_ref[:, td : td + r]
    packed_ref[:, 0:td] = proj
    packed_ref[:, td : td + r] = gram


def start_of(sz, k):
    me = lax.axis_index("tiles") & (sz.group - 1)
    return pl.multiple_of((me ^ k) * sz.chunk, BLOCK)


def first_projection(sz, f_hbm, b_hbm, d_hbm, valid_hbm, fore_hbm, f_ref, packed_ref, own_ref, least_ref, bar_ref, valid_ref, *refs):
    stack_refs, (b_ref, d_ref, flags_ref, sems) = refs[: sz.group], refs[sz.group :]
    small = [
        pltpu.make_async_copy(d_hbm, d_ref, sems.at[0]),
        pltpu.make_async_copy(b_hbm, b_ref, sems.at[1]),
        pltpu.make_async_copy(valid_hbm, flags_ref.at[0:1], sems.at[2]),
        pltpu.make_async_copy(fore_hbm, flags_ref.at[8:9], sems.at[3]),
    ]
    spans = [pl.ds(start_of(sz, k), sz.chunk) for k in range(sz.group)]
    large = [pltpu.make_async_copy(f_hbm.at[:, s], f_ref.at[:, s], sems.at[4 + k]) for k, s in enumerate(spans)]
    for copy in small + large:
        copy.start()
    for copy in small[:2]:
        copy.wait()
    me = lax.axis_index("tiles") & (sz.group - 1)
    own_ref[:, 0 : sz.chunk] = b_ref[:, spans[0]]
    own_ref[:, sz.chunk :] = jnp.zeros((sz.rank, sz.extra), F32)
    for j in range(sz.blocks):
        own_ref[j % sz.rank, pl.ds(sz.chunk + j // sz.rank * BLOCK, BLOCK)] = d_ref[me * sz.blocks + j, :]
    bases = [b_ref[:, span] for span in spans]
    darks = [[d_ref[pl.ds((me ^ k) * sz.blocks + j, 1), :] for j in range(sz.blocks)] for k in range(sz.group)]
    for k in range(sz.group):
        stack_block(sz, stack_refs[k], bases[k], darks[k])
    parts = [ref[0 : 3 * sz.rank, :] for ref in stack_refs]
    gram = tree([lax.dot_general(p, p, NT, preferred_element_type=F32) for p in parts])
    dark = tree([b[:, j * BLOCK : (j + 1) * BLOCK] * d for b, rows in zip(bases, darks) for j, d in enumerate(rows)])
    for copy in small[2:]:
        copy.wait()
    valid = flags_ref[0:1, :] != 0
    valid_ref[...] = jnp.broadcast_to(valid.astype(F32), valid_ref.shape)
    least = jnp.broadcast_to(jnp.where(valid, flags_ref[8:9, :], ROW_PX), (BLOCK, sz.tile_dev)).T
    least_ref[...] = least
    for block in range(bar_ref.shape[0]):
        bar_ref[block] = jnp.where(least <= block, 1.0, jnp.inf)
    for copy in large:
        copy.wait()
    proj = tree([lax.dot_general(p, f_ref[:, s], NT, preferred_element_type=F32) for p, s in zip(parts, spans)])
    pack_projections(sz, (proj, gram, dark), packed_ref)


def later_projection(sz, k, f_ref, chunk_ref, *refs):
    before_ref, packed_ref, stack_ref = refs if len(refs) == 3 else (None,) + refs
    d_rows = []
    for j in range(sz.blocks):
        lane = sz.chunk + j // sz.rank * BLOCK
        d_rows.append(chunk_ref[j % sz.rank : j % sz.rank + 1, lane : lane + BLOCK])
    frames = f_ref[:, pl.ds(start_of(sz, k), sz.chunk)]
    totals = project_chunk(sz, frames, stack_ref, chunk_ref[:, 0 : sz.chunk], d_rows, None)
    pack_projections(sz, totals, packed_ref, before_ref)


def residual(sz, f_ref, stack_ref, parts, start, step, width):
    model = lax.dot_general(
        parts, stack_ref[:, step * width : (step + 1) * width], NN, preferred_element_type=F32
    )
    return f_ref[:, pl.ds(pl.multiple_of(start + step * width, BLOCK), width)].astype(F32) - model


def solve_tiles(sz, width, *refs):
    packed = refs[: sz.n_pix]
    stack_refs, refs = refs[sz.n_pix : sz.n_pix + sz.group], refs[sz.n_pix + sz.group :]
    f_ref, least_ref, valid_ref, coef_ref, three_ref, parts_ref, note_ref = refs
    r, td = sz.rank, sz.tile_dev
    a = tree([ref[...] for ref in packed]) / sz.pixels_all
    gram = a[:, td : td + r] + RIDGE * eye_at((r, r), 0)
    sides = [a[:, at : at + BLOCK] for at in range(0, td, BLOCK)]
    coef = jnp.concatenate(solve_spd(gram, sides), axis=1)
    coef_ref[...] = coef
    hi, mid, low = split3(coef)
    three_ref[...] = jnp.concatenate([hi, mid, jnp.ones((16, td), BF16), low], axis=0)
    row = lax.broadcasted_iota(jnp.int32, (BLOCK - 6 * r, td), 0)
    ones = (row < 3).astype(F32)
    hi, mid, low = hi.astype(F32), mid.astype(F32), low.astype(F32)
    parts = jnp.concatenate([hi, hi, hi, mid, mid, low, ones], axis=0).T.astype(BF16)
    parts_ref[...] = parts
    parts = parts[:, 0 : sz.stack]
    least = least_ref[...]

    total = jnp.zeros((8, BLOCK), F32)
    for k, stack_ref in enumerate(stack_refs):
        start = start_of(sz, k)
        for step in range(sz.chunk // width):
            res = residual(sz, f_ref, stack_ref, parts, start, step, width)
            square = res * res
            for j in range(width // BLOCK):
                block = (start // BLOCK + step * (width // BLOCK) + j) % (ROW_PX // BLOCK)
                term = jnp.where(least <= block, square[:, j * BLOCK : (j + 1) * BLOCK], 0.0)
                total = total + jnp.sum(term.reshape(td // 8, 8, BLOCK), axis=0)
    total = jnp.sum(jnp.sum(total, axis=0, keepdims=True), axis=1, keepdims=True)
    products = jnp.concatenate([coef[i : i + 1] * coef for i in range(r)], axis=0)
    ones = valid_ref[...].astype(BF16)
    flat = sum(lax.dot_general(ones, part, NT, preferred_element_type=F32) for part in split3(products))
    lane = lax.broadcasted_iota(jnp.int32, flat.shape, 1)
    flat = jnp.where(lane == sz.spot, total, flat)
    for at in range(0, note_ref.shape[0], 8):
        note_ref[at : at + 8, :] = flat


def invert_gram(sz, note_ref, inverse_ref):
    r = sz.rank
    flat = jnp.sum(note_ref[...], axis=0, keepdims=True)
    gram = jnp.concatenate([flat[:, i * r : (i + 1) * r] for i in range(r)], axis=0)
    row = lax.broadcasted_iota(jnp.int32, (r, r), 0)
    col = lax.broadcasted_iota(jnp.int32, (r, r), 1)
    twin = flat[:, sz.twin : sz.twin + 1]
    gram = jnp.where((row == r - 1) & (col == r - 2), twin, gram)
    gram = gram / (sz.n_pix * sz.tiles_all) + RIDGE * eye_at((r, r), 0)
    (inverse_ref[...],) = solve_spd(gram, [eye_at((r, BLOCK), 0)])


def update_terms(sz, width, ks, note_ref, f_ref, bar_ref, three_ref, parts_ref, *refs):
    r = sz.rank
    total = jnp.sum(note_ref[:, sz.spot : sz.spot + 1], axis=0, keepdims=True)
    spread = total / (sz.tiles_all * sz.pixels_all) + 1e-05
    scale = jnp.broadcast_to(1.0 / (4.0 * spread), (8, BLOCK))[0:1, :]
    for k, stack_ref, out_ref in zip(ks, refs[: len(ks)], refs[len(ks) :]):
        chunk_terms(sz, width, k, scale, f_ref, stack_ref, bar_ref, three_ref, parts_ref, out_ref)


def chunk_terms(sz, width, k, scale, f_ref, stack_ref, bar_ref, three_ref, parts_ref, out_ref):
    r = sz.rank
    start = start_of(sz, k)
    parts = parts_ref[:, 0 : sz.stack]
    three = three_ref[...]
    two = three[0 : 2 * r + 16]
    each = width // BLOCK

    def place(flat):
        lane = sz.chunk + flat // r * BLOCK
        return slice(flat % r, flat % r + 1), slice(lane, lane + BLOCK)

    for step in range(sz.chunk // width):
        res = residual(sz, f_ref, stack_ref, parts, start, step, width)
        hi_parts, mid_parts = [], []
        for j in range(each):
            block = (start // BLOCK + step * each + j) % (ROW_PX // BLOCK)
            x = res[:, j * BLOCK : (j + 1) * BLOCK]
            g = pl.reciprocal(x * x * scale + bar_ref[jnp.minimum(block, bar_ref.shape[0] - 1)], approx=True)
            out_ref[place(sz.blocks + step * each + j)] = jnp.sum(g, axis=0, keepdims=True)
            w = g * x
            w_hi = w.astype(BF16)
            hi_parts.append(w_hi)
            mid_parts.append((w - w_hi.astype(F32)).astype(BF16))
        terms = lax.dot_general(three, jnp.concatenate(hi_parts, axis=1), NN, preferred_element_type=F32)
        more = lax.dot_general(two, jnp.concatenate(mid_parts, axis=1), NN, preferred_element_type=F32)
        out_ref[:, step * width : (step + 1) * width] = terms[0:r] + (
            terms[r : 2 * r] + terms[2 * r + 16 :] + more[0:r] + more[r : 2 * r]
        )
        sums = terms[2 * r : 2 * r + 1] + more[2 * r : 2 * r + 1]
        for j in range(each):
            out_ref[place(step * each + j)] = sums[:, j * BLOCK : (j + 1) * BLOCK]
    used = 2 * sz.blocks
    if used % r:
        out_ref[used % r :, sz.chunk + used // r * BLOCK :] = jnp.zeros((r - used % r, BLOCK), F32)


def update_chunk(sz, places, inverse_ref, old_ref, *refs):
    total_refs, new_ref = refs[:-1], refs[-1]
    r = sz.rank
    totals = tree([total_refs[i][...] for i in places])
    inverse = inverse_ref[:, 0:r]
    change = jnp.dot(inverse, totals[:, 0 : sz.chunk] / sz.tiles_all, precision=lax.Precision.HIGHEST, preferred_element_type=F32)
    new_ref[:, 0 : sz.chunk] = old_ref[:, 0 : sz.chunk] + change
    new_ref[:, sz.chunk :] = jnp.zeros((r, sz.extra), F32)

    def place(flat):
        return flat % r, sz.chunk + flat // r * BLOCK

    many = 8 if sz.blocks % 8 == 0 else 1
    for j in range(0, sz.blocks, many):
        (row, lane), (row_g, lane_g) = place(j), place(sz.blocks + j)
        w = totals[row : row + many, lane : lane + BLOCK]
        g = totals[row_g : row_g + many, lane_g : lane_g + BLOCK]
        new_ref[row : row + many, lane : lane + BLOCK] = (
            old_ref[row : row + many, lane : lane + BLOCK] + w / (g + 1.0)
        )


def assemble(sz, ks, coef_ref, *refs):
    chunks, (b_ref, d_ref, coef_out_ref) = refs[: sz.group], refs[sz.group :]
    coef_out_ref[...] = coef_ref[...]
    me = lax.axis_index("tiles") & (sz.group - 1)
    for k, ref in zip(ks, chunks):
        c = me ^ k
        b_ref[:, pl.ds(pl.multiple_of(c * sz.chunk, BLOCK), sz.chunk)] = ref[:, 0 : sz.chunk]
        for j in range(sz.blocks):
            lane = sz.chunk + j // sz.rank * BLOCK
            d_ref[c * sz.blocks + j, :] = ref[j % sz.rank, lane : lane + BLOCK]


def call(body, outs, ins, in_hbm=False, scratch=()):
    return pl.pallas_call(
        body,
        out_shape=[jax.ShapeDtypeStruct(s, t) for s, t in outs],
        in_specs=[pl.BlockSpec(memory_space=pltpu.HBM)] * len(ins) if in_hbm else vmem(len(ins)),
        out_specs=vmem(len(outs)),
        scratch_shapes=scratch,
        compiler_params=params(),
    )(*([pltpu.with_memory_space_constraint(x, pltpu.HBM) for x in ins] if in_hbm else ins))


def local(frames, tile_valid, foreground_blocks, basis_start, dark_start):
    td, pd = frames.shape
    r = basis_start.shape[0]
    sz = Sizes(td, pd, r, lax.axis_size("tiles"), lax.axis_size("pix"))
    everyone = ("tiles", "pix")
    devices = sz.n_tiles * sz.n_pix
    pix_masks = range(1, sz.n_pix)
    width = min(256, sz.chunk)
    chunk_shape = (r, sz.chunk + sz.extra)
    packed_out = ((r, td + BLOCK), F32)
    stack_out = ((sz.stack, sz.chunk), BF16)
    masks = sz.tile_levels[0]
    for iteration in range(ITERS):
        if iteration == 0:
            frames, packed, old, least, bar, valid, *stacks = call(
                functools.partial(first_projection, sz),
                [((td, pd), BF16), packed_out, (chunk_shape, F32), ((td, BLOCK), jnp.int32), ((ROW_PX // BLOCK // 2 + 1, td, BLOCK), F32), ((8, td), F32)]
                + [stack_out] * sz.group,
                [frames, basis_start, dark_start.reshape(pd // BLOCK, BLOCK), tile_valid.reshape(1, td), foreground_blocks.reshape(1, td)],
                in_hbm=True,
                scratch=[
                    pltpu.VMEM((r, pd), F32),
                    pltpu.VMEM((pd // BLOCK, BLOCK), F32),
                    pltpu.VMEM((16, td), jnp.int32),
                    pltpu.SemaphoreType.DMA((4 + sz.group,)),
                ],
            )
        else:
            before, stacks = [], [None] * sz.group
            for k in [0] + permuted(masks, ORDER[2]):
                packed, stacks[k] = call(
                    functools.partial(later_projection, sz, k), [packed_out, stack_out], [frames, chunks[k]] + before
                )
                before = [packed]
        both = [packed] + [partner(packed, "pix", m) for m in pix_masks]
        coef, three, parts, note = call(
            functools.partial(solve_tiles, sz, width),
            [((r, td), F32), ((3 * r + 16, td), BF16), ((td, BLOCK), BF16), ((devices, r * r), F32)],
            both + stacks + [frames, least, valid],
        )
        notes = lax.all_to_all(note, everyone, 0, 0, tiled=True)
        (inverse,) = call(functools.partial(invert_gram, sz), [((r, BLOCK), F32)], [notes])
        terms = {}
        for ks in (list(masks), [0]):
            outs = call(
                functools.partial(update_terms, sz, width, ks),
                [(chunk_shape, F32)] * len(ks),
                [notes, frames, bar, three, parts] + [stacks[k] for k in ks],
            )
            terms.update(zip(ks, outs))
        order = permuted(masks, ORDER[0])
        got = dict(zip(order, lax.optimization_barrier([partner(terms[m], "tiles", m) for m in order])))
        total = tree([terms[0]] + [got[m] for m in masks])
        later = sz.tile_levels[1:]
        for level in later[:-1]:
            total = sum_level(total, "tiles", level)
        last = later[-1] if later else ()
        order = permuted(last, ORDER[1])
        swap = {last[0]: last[1], last[1]: last[0]} if len(last) == 3 else {}
        totals = [total] + [crossed(total, m, swap) for m in order]
        places = [0] + [1 + order.index(m) for m in last]
        (old,) = call(functools.partial(update_chunk, sz, places), [(chunk_shape, F32)], [inverse, old] + totals)
        chunks = [old] + [partner(old, "tiles", m) for m in masks]
    ks = [0] + permuted(masks, ORDER[3])
    basis, dark, coef = call(
        functools.partial(assemble, sz, ks),
        [((r, pd), F32), ((pd // BLOCK, BLOCK), F32), ((r, td), F32)],
        [coef] + [chunks[k] for k in ks],
    )
    return basis, dark.reshape(pd), coef.T


def solution(mesh):
    return jax.shard_map(
        local,
        mesh=mesh,
        in_specs=(P("tiles", "pix"), P("tiles"), P("tiles"), P(None, "pix"), P("pix")),
        out_specs=(P(None, "pix"), P("pix"), P("tiles", None)),
        check_vma=False,
    )
```

```python
import functools

import jax
import jax.numpy as jnp
from jax import lax
from jax.experimental import pallas as pl
from jax.experimental.pallas import tpu as pltpu
from jax.sharding import PartitionSpec as P

ROW_PX = 2048
BLOCK = 128
ITERS = 2
RIDGE = 0.01
VMEM_LIMIT = 48 * 1024 * 1024

F32 = jnp.float32
BF16 = jnp.bfloat16
NN = (((1,), (0,)), ((), ()))
NT = (((1,), (1,)), ((), ()))


def params():
    return pltpu.CompilerParams(vmem_limit_bytes=VMEM_LIMIT)


def vmem(n):
    return [pl.BlockSpec(memory_space=pltpu.VMEM)] * n


SMEM = pl.BlockSpec(memory_space=pltpu.SMEM)


def split3(x):
    hi = x.astype(BF16)
    rest = x - hi.astype(F32)
    mid = rest.astype(BF16)
    low = (rest - mid.astype(F32)).astype(BF16)
    return hi, mid, low


def solve_spd(gram, sides):
    r = gram.shape[0]
    columns = [jnp.broadcast_to(gram[:, j : j + 1], (r, BLOCK)) for j in range(r)]
    rows = lax.broadcasted_iota(jnp.int32, (r, BLOCK), 0)
    for k in range(r):
        pivot = columns[k]
        inverse = 1.0 / pivot[k : k + 1, :]

        def step(x):
            scaled = x[k : k + 1, :] * inverse
            return jnp.where(rows == k, scaled, x - pivot * scaled)

        columns = columns[: k + 1] + [step(c) for c in columns[k + 1 :]]
        sides = [step(x) for x in sides]
    return sides


def eye_at(shape, first):
    row = lax.broadcasted_iota(jnp.int32, shape, 0)
    col = lax.broadcasted_iota(jnp.int32, shape, 1)
    return (col == row + first).astype(F32)


ORDER = ((0, 1, 2), (2, 0, 1), (2, 1, 0), (2, 1, 0))


def permuted(masks, order):
    return [masks[i] for i in order] if len(masks) == 3 else list(masks)


class Sizes:
    def __init__(self, tile_dev, pix_dev, rank, n_tiles, n_pix):
        self.tile_dev, self.pix_dev, self.rank = tile_dev, pix_dev, rank
        self.n_tiles, self.n_pix = n_tiles, n_pix
        self.tiles_all, self.pixels_all = tile_dev * n_tiles, pix_dev * n_pix
        self.tile_levels = levels(n_tiles)
        self.group = len(self.tile_levels[0]) + 1 if self.tile_levels else 1
        self.chunk = pix_dev // self.group
        self.blocks = self.chunk // BLOCK
        self.extra = BLOCK * (-(-2 * self.blocks // rank))
        self.stack = 6 * rank + 16
        self.spot, self.twin = rank * rank - 2, rank * rank - rank - 1


def levels(n):
    if n & (n - 1):
        return None
    out, bit = [], 1
    while bit < n:
        out.append((bit, 2 * bit, 3 * bit) if 4 * bit <= n else (bit,))
        bit *= 4
    return out


def partner(x, axis, mask):
    n = lax.axis_size(axis)
    return lax.ppermute(x, axis, [(i, i ^ mask) for i in range(n)])


def crossed(x, mask, swap):
    n, cores = lax.axis_size("tiles"), lax.axis_size("pix")
    pairs = []
    for i in range(n):
        for p in range(cores):
            pairs.append((i * cores + p, (i ^ (swap.get(mask, mask) if p & 1 else mask)) * cores + p))
    return lax.ppermute(x, ("tiles", "pix"), pairs)


def tree(parts):
    while len(parts) > 1:
        parts = [a + b for a, b in zip(parts[::2], parts[1::2])]
    return parts[0]


def sum_level(x, axis, masks):
    return tree([x] + [partner(x, axis, m) for m in masks])


def stack_block(sz, stack_ref, b, d_rows):
    r = sz.rank
    hi, mid, low = split3(b)
    for at, part in enumerate((hi, mid, low, hi, mid, hi)):
        stack_ref[at * r : (at + 1) * r, :] = part
    row = lax.broadcasted_iota(jnp.int32, (16, BLOCK), 0)
    for j, d in enumerate(d_rows):
        d_hi, d_mid, d_low = (part.astype(F32) for part in split3(d))
        tile = jnp.where(row == 0, d_hi, jnp.where(row == 1, d_mid, jnp.where(row == 2, d_low, 0.0)))
        stack_ref[6 * r : 6 * r + 16, j * BLOCK : (j + 1) * BLOCK] = tile.astype(BF16)


def project_chunk(sz, frames, stack_ref, b, d_rows, totals):
    r = sz.rank
    stack_block(sz, stack_ref, b, d_rows)
    parts = stack_ref[0 : 3 * r, :]
    proj = lax.dot_general(parts, frames, NT, preferred_element_type=F32)
    gram = lax.dot_general(parts, parts, NT, preferred_element_type=F32)
    dark = tree([b[:, j * BLOCK : (j + 1) * BLOCK] * d for j, d in enumerate(d_rows)])
    new = (proj, gram, dark)
    return new if totals is None else tuple(a + b for a, b in zip(totals, new))


def pack_projections(sz, totals, packed_ref, before_ref=None):
    r, td = sz.rank, sz.tile_dev
    proj, gram, dark = totals
    proj = proj[0:r] + proj[r : 2 * r] + proj[2 * r : 3 * r] - jnp.sum(dark, axis=1, keepdims=True)
    gram = gram[0:r] + gram[r : 2 * r] + gram[2 * r : 3 * r]
    gram = gram[:, 0:r] + gram[:, r : 2 * r] + gram[:, 2 * r : 3 * r]
    if before_ref is None:
        packed_ref[:, td : td + BLOCK] = jnp.zeros((r, BLOCK), F32)
    else:
        proj = proj + before_ref[:, 0:td]
        packed_ref[:, td : td + BLOCK] = before_ref[:, td : td + BLOCK]
        gram = gram + before_ref[:, td : td + r]
    packed_ref[:, 0:td] = proj
    packed_ref[:, td : td + r] = gram


def start_of(sz, k):
    me = lax.axis_index("tiles") & (sz.group - 1)
    return pl.multiple_of((me ^ k) * sz.chunk, BLOCK)


def first_projection(sz, f_hbm, b_hbm, d_hbm, valid_hbm, fore_hbm, f_ref, packed_ref, own_ref, least_ref, valid_ref, *refs):
    stack_refs, (b_ref, d_ref, flags_ref, sems) = refs[: sz.group], refs[sz.group :]
    small = [
        pltpu.make_async_copy(d_hbm, d_ref, sems.at[0]),
        pltpu.make_async_copy(b_hbm, b_ref, sems.at[1]),
        pltpu.make_async_copy(valid_hbm, flags_ref.at[0:1], sems.at[2]),
        pltpu.make_async_copy(fore_hbm, flags_ref.at[8:9], sems.at[3]),
    ]
    spans = [pl.ds(start_of(sz, k), sz.chunk) for k in range(sz.group)]
    large = [pltpu.make_async_copy(f_hbm.at[:, s], f_ref.at[:, s], sems.at[4 + k]) for k, s in enumerate(spans)]
    for copy in small + large:
        copy.start()
    for copy in small[:2]:
        copy.wait()
    me = lax.axis_index("tiles") & (sz.group - 1)
    own_ref[:, 0 : sz.chunk] = b_ref[:, spans[0]]
    own_ref[:, sz.chunk :] = jnp.zeros((sz.rank, sz.extra), F32)
    for j in range(sz.blocks):
        own_ref[j % sz.rank, pl.ds(sz.chunk + j // sz.rank * BLOCK, BLOCK)] = d_ref[me * sz.blocks + j, :]
    bases = [b_ref[:, span] for span in spans]
    darks = [[d_ref[pl.ds((me ^ k) * sz.blocks + j, 1), :] for j in range(sz.blocks)] for k in range(sz.group)]
    for k in range(sz.group):
        stack_block(sz, stack_refs[k], bases[k], darks[k])
    parts = [ref[0 : 3 * sz.rank, :] for ref in stack_refs]
    gram = tree([lax.dot_general(p, p, NT, preferred_element_type=F32) for p in parts])
    dark = tree([b[:, j * BLOCK : (j + 1) * BLOCK] * d for b, rows in zip(bases, darks) for j, d in enumerate(rows)])
    for copy in small[2:]:
        copy.wait()
    valid = flags_ref[0:1, :] != 0
    valid_ref[...] = jnp.broadcast_to(valid.astype(F32), valid_ref.shape)
    least_ref[...] = jnp.where(valid, flags_ref[8:9, :], ROW_PX) + jnp.zeros(least_ref.shape, jnp.int32)
    for copy in large:
        copy.wait()
    proj = tree([lax.dot_general(p, f_ref[:, s], NT, preferred_element_type=F32) for p, s in zip(parts, spans)])
    pack_projections(sz, (proj, gram, dark), packed_ref)


def make_masks(least_ref, keep_ref, bar_ref):
    least = jnp.broadcast_to(least_ref[0:1, :], (BLOCK, least_ref.shape[1])).T
    for block in range(bar_ref.shape[0]):
        usable = least <= block
        keep_ref[block] = jnp.where(usable, 1.0, 0.0)
        bar_ref[block] = jnp.where(usable, 1.0, jnp.inf)


def later_projection(sz, k, f_ref, chunk_ref, *refs):
    before_ref, packed_ref, stack_ref = refs if len(refs) == 3 else (None,) + refs
    d_rows = []
    for j in range(sz.blocks):
        lane = sz.chunk + j // sz.rank * BLOCK
        d_rows.append(chunk_ref[j % sz.rank : j % sz.rank + 1, lane : lane + BLOCK])
    frames = f_ref[:, pl.ds(start_of(sz, k), sz.chunk)]
    totals = project_chunk(sz, frames, stack_ref, chunk_ref[:, 0 : sz.chunk], d_rows, None)
    pack_projections(sz, totals, packed_ref, before_ref)


def residual(sz, f_ref, stack_ref, parts, start, step, width):
    model = lax.dot_general(
        parts, stack_ref[:, step * width : (step + 1) * width], NN, preferred_element_type=F32
    )
    return f_ref[:, pl.ds(pl.multiple_of(start + step * width, BLOCK), width)].astype(F32) - model


def solve_tiles(sz, width, *refs):
    packed = refs[: sz.n_pix]
    stack_refs, refs = refs[sz.n_pix : sz.n_pix + sz.group], refs[sz.n_pix + sz.group :]
    f_ref, keep_ref, valid_ref, coef_ref, three_ref, parts_ref, note_ref = refs
    r, td = sz.rank, sz.tile_dev
    a = tree([ref[...] for ref in packed]) / sz.pixels_all
    gram = a[:, td : td + r] + RIDGE * eye_at((r, r), 0)
    sides = [a[:, at : at + BLOCK] for at in range(0, td, BLOCK)]
    coef = jnp.concatenate(solve_spd(gram, sides), axis=1)
    coef_ref[...] = coef
    hi, mid, low = split3(coef)
    three_ref[...] = jnp.concatenate([hi, mid, jnp.ones((16, td), BF16), low], axis=0)
    row = lax.broadcasted_iota(jnp.int32, (BLOCK - 6 * r, td), 0)
    ones = (row < 3).astype(F32)
    hi, mid, low = hi.astype(F32), mid.astype(F32), low.astype(F32)
    parts = jnp.concatenate([hi, hi, hi, mid, mid, low, ones], axis=0).T.astype(BF16)
    parts_ref[...] = parts
    parts = parts[:, 0 : sz.stack]

    total = jnp.zeros((8, BLOCK), F32)
    for k, stack_ref in enumerate(stack_refs):
        start = start_of(sz, k)
        for step in range(sz.chunk // width):
            res = residual(sz, f_ref, stack_ref, parts, start, step, width)
            square = res * res
            for j in range(width // BLOCK):
                block = (start // BLOCK + step * (width // BLOCK) + j) % (ROW_PX // BLOCK)
                keep = keep_ref[jnp.minimum(block, keep_ref.shape[0] - 1)]
                term = keep * square[:, j * BLOCK : (j + 1) * BLOCK]
                total = total + jnp.sum(term.reshape(td // 8, 8, BLOCK), axis=0)
    total = jnp.sum(jnp.sum(total, axis=0, keepdims=True), axis=1, keepdims=True)
    products = jnp.concatenate([coef[i : i + 1] * coef for i in range(r)], axis=0)
    ones = valid_ref[...].astype(BF16)
    flat = sum(lax.dot_general(ones, part, NT, preferred_element_type=F32) for part in split3(products))
    lane = lax.broadcasted_iota(jnp.int32, flat.shape, 1)
    flat = jnp.where(lane == sz.spot, total, flat)
    for at in range(0, note_ref.shape[0], 8):
        note_ref[at : at + 8, :] = flat


def invert_gram(sz, note_ref, inverse_ref):
    r = sz.rank
    flat = jnp.sum(note_ref[...], axis=0, keepdims=True)
    gram = jnp.concatenate([flat[:, i * r : (i + 1) * r] for i in range(r)], axis=0)
    row = lax.broadcasted_iota(jnp.int32, (r, r), 0)
    col = lax.broadcasted_iota(jnp.int32, (r, r), 1)
    twin = flat[:, sz.twin : sz.twin + 1]
    gram = jnp.where((row == r - 1) & (col == r - 2), twin, gram)
    gram = gram / (sz.n_pix * sz.tiles_all) + RIDGE * eye_at((r, r), 0)
    (inverse_ref[...],) = solve_spd(gram, [eye_at((r, BLOCK), 0)])


def update_terms(sz, width, ks, note_ref, f_ref, bar_ref, three_ref, parts_ref, *refs):
    r = sz.rank
    total = jnp.sum(note_ref[:, sz.spot : sz.spot + 1], axis=0, keepdims=True)
    spread = total / (sz.tiles_all * sz.pixels_all) + 1e-05
    scale = jnp.broadcast_to(1.0 / (4.0 * spread), (8, BLOCK))[0:1, :]
    for k, stack_ref, out_ref in zip(ks, refs[: len(ks)], refs[len(ks) :]):
        chunk_terms(sz, width, k, scale, f_ref, stack_ref, bar_ref, three_ref, parts_ref, out_ref)


def chunk_terms(sz, width, k, scale, f_ref, stack_ref, bar_ref, three_ref, parts_ref, out_ref):
    r = sz.rank
    start = start_of(sz, k)
    parts = parts_ref[:, 0 : sz.stack]
    three = three_ref[...]
    two = three[0 : 2 * r + 16]
    each = width // BLOCK

    def place(flat):
        lane = sz.chunk + flat // r * BLOCK
        return slice(flat % r, flat % r + 1), slice(lane, lane + BLOCK)

    for step in range(sz.chunk // width):
        res = residual(sz, f_ref, stack_ref, parts, start, step, width)
        hi_parts, mid_parts = [], []
        for j in range(each):
            block = (start // BLOCK + step * each + j) % (ROW_PX // BLOCK)
            x = res[:, j * BLOCK : (j + 1) * BLOCK]
            g = pl.reciprocal(x * x * scale + bar_ref[jnp.minimum(block, bar_ref.shape[0] - 1)], approx=True)
            out_ref[place(sz.blocks + step * each + j)] = jnp.sum(g, axis=0, keepdims=True)
            w = g * x
            w_hi = w.astype(BF16)
            hi_parts.append(w_hi)
            mid_parts.append((w - w_hi.astype(F32)).astype(BF16))
        terms = lax.dot_general(three, jnp.concatenate(hi_parts, axis=1), NN, preferred_element_type=F32)
        more = lax.dot_general(two, jnp.concatenate(mid_parts, axis=1), NN, preferred_element_type=F32)
        out_ref[:, step * width : (step + 1) * width] = terms[0:r] + (
            terms[r : 2 * r] + terms[2 * r + 16 :] + more[0:r] + more[r : 2 * r]
        )
        sums = terms[2 * r : 2 * r + 1] + more[2 * r : 2 * r + 1]
        for j in range(each):
            out_ref[place(step * each + j)] = sums[:, j * BLOCK : (j + 1) * BLOCK]
    used = 2 * sz.blocks
    if used % r:
        out_ref[used % r :, sz.chunk + used // r * BLOCK :] = jnp.zeros((r - used % r, BLOCK), F32)


def update_chunk(sz, places, inverse_ref, old_ref, *refs):
    total_refs, new_ref = refs[:-1], refs[-1]
    r = sz.rank
    totals = tree([total_refs[i][...] for i in places])
    inverse = inverse_ref[:, 0:r]
    change = jnp.dot(inverse, totals[:, 0 : sz.chunk] / sz.tiles_all, precision=lax.Precision.HIGHEST, preferred_element_type=F32)
    new_ref[:, 0 : sz.chunk] = old_ref[:, 0 : sz.chunk] + change
    new_ref[:, sz.chunk :] = jnp.zeros((r, sz.extra), F32)

    def place(flat):
        return flat % r, sz.chunk + flat // r * BLOCK

    many = 8 if sz.blocks % 8 == 0 else 1
    for j in range(0, sz.blocks, many):
        (row, lane), (row_g, lane_g) = place(j), place(sz.blocks + j)
        w = totals[row : row + many, lane : lane + BLOCK]
        g = totals[row_g : row_g + many, lane_g : lane_g + BLOCK]
        new_ref[row : row + many, lane : lane + BLOCK] = (
            old_ref[row : row + many, lane : lane + BLOCK] + w / (g + 1.0)
        )


def assemble(sz, ks, coef_ref, *refs):
    chunks, (b_ref, d_ref, coef_out_ref) = refs[: sz.group], refs[sz.group :]
    coef_out_ref[...] = coef_ref[...]
    me = lax.axis_index("tiles") & (sz.group - 1)
    for k, ref in zip(ks, chunks):
        c = me ^ k
        b_ref[:, pl.ds(pl.multiple_of(c * sz.chunk, BLOCK), sz.chunk)] = ref[:, 0 : sz.chunk]
        for j in range(sz.blocks):
            lane = sz.chunk + j // sz.rank * BLOCK
            d_ref[c * sz.blocks + j, :] = ref[j % sz.rank, lane : lane + BLOCK]


def call(body, outs, ins, in_hbm=False, scratch=()):
    return pl.pallas_call(
        body,
        out_shape=[jax.ShapeDtypeStruct(s, t) for s, t in outs],
        in_specs=[pl.BlockSpec(memory_space=pltpu.HBM)] * len(ins) if in_hbm else vmem(len(ins)),
        out_specs=vmem(len(outs)),
        scratch_shapes=scratch,
        compiler_params=params(),
    )(*([pltpu.with_memory_space_constraint(x, pltpu.HBM) for x in ins] if in_hbm else ins))


def local(frames, tile_valid, foreground_blocks, basis_start, dark_start):
    td, pd = frames.shape
    r = basis_start.shape[0]
    sz = Sizes(td, pd, r, lax.axis_size("tiles"), lax.axis_size("pix"))
    everyone = ("tiles", "pix")
    devices = sz.n_tiles * sz.n_pix
    pix_masks = range(1, sz.n_pix)
    width = min(256, sz.chunk)
    chunk_shape = (r, sz.chunk + sz.extra)
    packed_out = ((r, td + BLOCK), F32)
    stack_out = ((sz.stack, sz.chunk), BF16)
    masks = sz.tile_levels[0]
    for iteration in range(ITERS):
        if iteration == 0:
            frames, packed, old, least, valid, *stacks = call(
                functools.partial(first_projection, sz),
                [((td, pd), BF16), packed_out, (chunk_shape, F32), ((8, td), jnp.int32), ((8, td), F32)]
                + [stack_out] * sz.group,
                [frames, basis_start, dark_start.reshape(pd // BLOCK, BLOCK), tile_valid.reshape(1, td), foreground_blocks.reshape(1, td)],
                in_hbm=True,
                scratch=[
                    pltpu.VMEM((r, pd), F32),
                    pltpu.VMEM((pd // BLOCK, BLOCK), F32),
                    pltpu.VMEM((16, td), jnp.int32),
                    pltpu.SemaphoreType.DMA((4 + sz.group,)),
                ],
            )
        else:
            before, stacks = [], [None] * sz.group
            for k in [0] + permuted(masks, ORDER[2]):
                packed, stacks[k] = call(
                    functools.partial(later_projection, sz, k), [packed_out, stack_out], [frames, chunks[k]] + before
                )
                before = [packed]
        if iteration == 0:
            mask = ((ROW_PX // BLOCK // 2 + 1, td, BLOCK), F32)
            keep, bar = call(make_masks, [mask, mask], [least])
        both = [packed] + [partner(packed, "pix", m) for m in pix_masks]
        coef, three, parts, note = call(
            functools.partial(solve_tiles, sz, width),
            [((r, td), F32), ((3 * r + 16, td), BF16), ((td, BLOCK), BF16), ((devices, r * r), F32)],
            both + stacks + [frames, keep, valid],
        )
        notes = lax.all_to_all(note, everyone, 0, 0, tiled=True)
        (inverse,) = call(functools.partial(invert_gram, sz), [((r, BLOCK), F32)], [notes])
        terms = {}
        for ks in (list(masks), [0]):
            outs = call(
                functools.partial(update_terms, sz, width, ks),
                [(chunk_shape, F32)] * len(ks),
                [notes, frames, bar, three, parts] + [stacks[k] for k in ks],
            )
            terms.update(zip(ks, outs))
        order = permuted(masks, ORDER[0])
        got = dict(zip(order, lax.optimization_barrier([partner(terms[m], "tiles", m) for m in order])))
        total = tree([terms[0]] + [got[m] for m in masks])
        later = sz.tile_levels[1:]
        for level in later[:-1]:
            total = sum_level(total, "tiles", level)
        last = later[-1] if later else ()
        order = permuted(last, ORDER[1])
        swap = {last[0]: last[1], last[1]: last[0]} if len(last) == 3 else {}
        totals = [total] + [crossed(total, m, swap) for m in order]
        places = [0] + [1 + order.index(m) for m in last]
        (old,) = call(functools.partial(update_chunk, sz, places), [(chunk_shape, F32)], [inverse, old] + totals)
        chunks = [old] + [partner(old, "tiles", m) for m in masks]
    ks = [0] + permuted(masks, ORDER[3])
    basis, dark, coef = call(
        functools.partial(assemble, sz, ks),
        [((r, pd), F32), ((pd // BLOCK, BLOCK), F32), ((r, td), F32)],
        [coef] + [chunks[k] for k in ks],
    )
    return basis, dark.reshape(pd), coef.T


def solution(mesh):
    return jax.shard_map(
        local,
        mesh=mesh,
        in_specs=(P("tiles", "pix"), P("tiles"), P("tiles"), P(None, "pix"), P("pix")),
        out_specs=(P(None, "pix"), P("pix"), P("tiles", None)),
        check_vma=False,
    )
```

```python
import functools

import jax
import jax.numpy as jnp
from jax import lax
from jax.experimental import pallas as pl
from jax.experimental.pallas import tpu as pltpu
from jax.sharding import PartitionSpec as P

ROW_PX = 2048
BLOCK = 128
ITERS = 2
RIDGE = 0.01
VMEM_LIMIT = 48 * 1024 * 1024

F32 = jnp.float32
BF16 = jnp.bfloat16
NN = (((1,), (0,)), ((), ()))
NT = (((1,), (1,)), ((), ()))


def params():
    return pltpu.CompilerParams(vmem_limit_bytes=VMEM_LIMIT)


def vmem(n):
    return [pl.BlockSpec(memory_space=pltpu.VMEM)] * n


SMEM = pl.BlockSpec(memory_space=pltpu.SMEM)


def split3(x):
    hi = x.astype(BF16)
    rest = x - hi.astype(F32)
    mid = rest.astype(BF16)
    low = (rest - mid.astype(F32)).astype(BF16)
    return hi, mid, low


def solve_spd(gram, sides):
    r = gram.shape[0]
    columns = [jnp.broadcast_to(gram[:, j : j + 1], (r, BLOCK)) for j in range(r)]
    rows = lax.broadcasted_iota(jnp.int32, (r, BLOCK), 0)
    for k in range(r):
        pivot = columns[k]
        inverse = 1.0 / pivot[k : k + 1, :]

        def step(x):
            scaled = x[k : k + 1, :] * inverse
            return jnp.where(rows == k, scaled, x - pivot * scaled)

        columns = columns[: k + 1] + [step(c) for c in columns[k + 1 :]]
        sides = [step(x) for x in sides]
    return sides


def eye_at(shape, first):
    row = lax.broadcasted_iota(jnp.int32, shape, 0)
    col = lax.broadcasted_iota(jnp.int32, shape, 1)
    return (col == row + first).astype(F32)


ORDER = ((0, 1, 2), (2, 0, 1), (2, 1, 0), (2, 1, 0))


def permuted(masks, order):
    return [masks[i] for i in order] if len(masks) == 3 else list(masks)


class Sizes:
    def __init__(self, tile_dev, pix_dev, rank, n_tiles, n_pix):
        self.tile_dev, self.pix_dev, self.rank = tile_dev, pix_dev, rank
        self.n_tiles, self.n_pix = n_tiles, n_pix
        self.tiles_all, self.pixels_all = tile_dev * n_tiles, pix_dev * n_pix
        self.tile_levels = levels(n_tiles)
        self.group = len(self.tile_levels[0]) + 1 if self.tile_levels else 1
        self.chunk = pix_dev // self.group
        self.blocks = self.chunk // BLOCK
        self.extra = BLOCK * (-(-2 * self.blocks // rank))
        self.stack = 6 * rank + 16
        self.spot, self.twin = rank * rank - 2, rank * rank - rank - 1


def levels(n):
    if n & (n - 1):
        return None
    out, bit = [], 1
    while bit < n:
        out.append((bit, 2 * bit, 3 * bit) if 4 * bit <= n else (bit,))
        bit *= 4
    return out


def partner(x, axis, mask):
    n = lax.axis_size(axis)
    return lax.ppermute(x, axis, [(i, i ^ mask) for i in range(n)])


def crossed(x, mask, swap):
    n, cores = lax.axis_size("tiles"), lax.axis_size("pix")
    pairs = []
    for i in range(n):
        for p in range(cores):
            pairs.append((i * cores + p, (i ^ (swap.get(mask, mask) if p & 1 else mask)) * cores + p))
    return lax.ppermute(x, ("tiles", "pix"), pairs)


def tree(parts):
    while len(parts) > 1:
        parts = [a + b for a, b in zip(parts[::2], parts[1::2])]
    return parts[0]


def sum_level(x, axis, masks):
    return tree([x] + [partner(x, axis, m) for m in masks])


def stack_block(sz, stack_ref, b, d_rows):
    r = sz.rank
    hi, mid, low = split3(b)
    for at, part in enumerate((hi, mid, low, hi, mid, hi)):
        stack_ref[at * r : (at + 1) * r, :] = part
    row = lax.broadcasted_iota(jnp.int32, (16, BLOCK), 0)
    for j, d in enumerate(d_rows):
        d_hi, d_mid, d_low = (part.astype(F32) for part in split3(d))
        tile = jnp.where(row == 0, d_hi, jnp.where(row == 1, d_mid, jnp.where(row == 2, d_low, 0.0)))
        stack_ref[6 * r : 6 * r + 16, j * BLOCK : (j + 1) * BLOCK] = tile.astype(BF16)


def project_chunk(sz, frames, stack_ref, b, d_rows, totals):
    r = sz.rank
    stack_block(sz, stack_ref, b, d_rows)
    parts = stack_ref[0 : 3 * r, :]
    proj = lax.dot_general(parts, frames, NT, preferred_element_type=F32)
    gram = lax.dot_general(parts, parts, NT, preferred_element_type=F32)
    dark = tree([b[:, j * BLOCK : (j + 1) * BLOCK] * d for j, d in enumerate(d_rows)])
    new = (proj, gram, dark)
    return new if totals is None else tuple(a + b for a, b in zip(totals, new))


def pack_projections(sz, totals, packed_ref, before_ref=None):
    r, td = sz.rank, sz.tile_dev
    proj, gram, dark = totals
    proj = proj[0:r] + proj[r : 2 * r] + proj[2 * r : 3 * r] - jnp.sum(dark, axis=1, keepdims=True)
    gram = gram[0:r] + gram[r : 2 * r] + gram[2 * r : 3 * r]
    gram = gram[:, 0:r] + gram[:, r : 2 * r] + gram[:, 2 * r : 3 * r]
    if before_ref is None:
        packed_ref[:, td : td + BLOCK] = jnp.zeros((r, BLOCK), F32)
    else:
        proj = proj + before_ref[:, 0:td]
        packed_ref[:, td : td + BLOCK] = before_ref[:, td : td + BLOCK]
        gram = gram + before_ref[:, td : td + r]
    packed_ref[:, 0:td] = proj
    packed_ref[:, td : td + r] = gram


def start_of(sz, k):
    me = lax.axis_index("tiles") & (sz.group - 1)
    return pl.multiple_of((me ^ k) * sz.chunk, BLOCK)


def first_projection(sz, f_hbm, b_hbm, d_hbm, valid_hbm, fore_hbm, f_ref, packed_ref, own_ref, least_ref, valid_ref, *refs):
    stack_refs, (b_ref, d_ref, flags_ref, sems) = refs[: sz.group], refs[sz.group :]
    small = [
        pltpu.make_async_copy(d_hbm, d_ref, sems.at[0]),
        pltpu.make_async_copy(b_hbm, b_ref, sems.at[1]),
        pltpu.make_async_copy(valid_hbm, flags_ref.at[0:1], sems.at[2]),
        pltpu.make_async_copy(fore_hbm, flags_ref.at[8:9], sems.at[3]),
    ]
    spans = [pl.ds(start_of(sz, k), sz.chunk) for k in range(sz.group)]
    large = [pltpu.make_async_copy(f_hbm.at[:, s], f_ref.at[:, s], sems.at[4 + k]) for k, s in enumerate(spans)]
    for copy in small + large:
        copy.start()
    for copy in small[:2]:
        copy.wait()
    me = lax.axis_index("tiles") & (sz.group - 1)
    own_ref[:, 0 : sz.chunk] = b_ref[:, spans[0]]
    own_ref[:, sz.chunk :] = jnp.zeros((sz.rank, sz.extra), F32)
    for j in range(sz.blocks):
        own_ref[j % sz.rank, pl.ds(sz.chunk + j // sz.rank * BLOCK, BLOCK)] = d_ref[me * sz.blocks + j, :]
    bases = [b_ref[:, span] for span in spans]
    darks = [[d_ref[pl.ds((me ^ k) * sz.blocks + j, 1), :] for j in range(sz.blocks)] for k in range(sz.group)]
    for k in range(sz.group):
        stack_block(sz, stack_refs[k], bases[k], darks[k])
    parts = [ref[0 : 3 * sz.rank, :] for ref in stack_refs]
    gram = tree([lax.dot_general(p, p, NT, preferred_element_type=F32) for p in parts])
    dark = tree([b[:, j * BLOCK : (j + 1) * BLOCK] * d for b, rows in zip(bases, darks) for j, d in enumerate(rows)])
    for copy in small[2:]:
        copy.wait()
    valid = flags_ref[0:1, :] != 0
    valid_ref[...] = jnp.broadcast_to(valid.astype(F32), valid_ref.shape)
    least_ref[...] = jnp.where(valid, flags_ref[8:9, :], ROW_PX) + jnp.zeros(least_ref.shape, jnp.int32)
    for copy in large:
        copy.wait()
    proj = tree([lax.dot_general(p, f_ref[:, s], NT, preferred_element_type=F32) for p, s in zip(parts, spans)])
    pack_projections(sz, (proj, gram, dark), packed_ref)


def make_masks(least_ref, keep_ref, bar_ref):
    least = jnp.broadcast_to(least_ref[0:1, :], (BLOCK, least_ref.shape[1])).T
    for block in range(bar_ref.shape[0]):
        usable = least <= block
        keep_ref[block] = jnp.where(usable, 1.0, 0.0)
        bar_ref[block] = jnp.where(usable, 1.0, jnp.inf)


def later_projection(sz, k, f_ref, chunk_ref, *refs):
    before_ref, packed_ref, stack_ref = refs if len(refs) == 3 else (None,) + refs
    d_rows = []
    for j in range(sz.blocks):
        lane = sz.chunk + j // sz.rank * BLOCK
        d_rows.append(chunk_ref[j % sz.rank : j % sz.rank + 1, lane : lane + BLOCK])
    frames = f_ref[:, pl.ds(start_of(sz, k), sz.chunk)]
    totals = project_chunk(sz, frames, stack_ref, chunk_ref[:, 0 : sz.chunk], d_rows, None)
    pack_projections(sz, totals, packed_ref, before_ref)


def residual(sz, f_ref, stack_ref, parts, start, step, width):
    model = lax.dot_general(
        parts, stack_ref[:, step * width : (step + 1) * width], NN, preferred_element_type=F32
    )
    return f_ref[:, pl.ds(pl.multiple_of(start + step * width, BLOCK), width)].astype(F32) - model


def solve_tiles(sz, width, *refs):
    packed = refs[: sz.n_pix]
    stack_refs, refs = refs[sz.n_pix : sz.n_pix + sz.group], refs[sz.n_pix + sz.group :]
    f_ref, keep_ref, valid_ref, coef_ref, three_ref, parts_ref, note_ref = refs
    r, td = sz.rank, sz.tile_dev
    a = tree([ref[...] for ref in packed]) / sz.pixels_all
    gram = a[:, td : td + r] + RIDGE * eye_at((r, r), 0)
    sides = [a[:, at : at + BLOCK] for at in range(0, td, BLOCK)]
    coef = jnp.concatenate(solve_spd(gram, sides), axis=1)
    coef_ref[...] = coef
    hi, mid, low = split3(coef)
    three_ref[...] = jnp.concatenate([hi, mid, jnp.ones((16, td), BF16), low], axis=0)
    row = lax.broadcasted_iota(jnp.int32, (BLOCK - 6 * r, td), 0)
    ones = (row < 3).astype(F32)
    hi, mid, low = hi.astype(F32), mid.astype(F32), low.astype(F32)
    parts = jnp.concatenate([hi, hi, hi, mid, mid, low, ones], axis=0).T.astype(BF16)
    parts_ref[...] = parts
    parts = parts[:, 0 : sz.stack]

    total = jnp.zeros((32, BLOCK), F32)
    for k, stack_ref in enumerate(stack_refs):
        start = start_of(sz, k)
        for step in range(sz.chunk // width):
            res = residual(sz, f_ref, stack_ref, parts, start, step, width)
            square = res * res
            for j in range(width // BLOCK):
                block = (start // BLOCK + step * (width // BLOCK) + j) % (ROW_PX // BLOCK)
                keep = keep_ref[jnp.minimum(block, keep_ref.shape[0] - 1)]
                term = keep * square[:, j * BLOCK : (j + 1) * BLOCK]
                total = total + jnp.sum(term.reshape(td // 32, 32, BLOCK), axis=0)
    total = jnp.sum(jnp.sum(total, axis=0, keepdims=True), axis=1, keepdims=True)
    products = jnp.concatenate([coef[i : i + 1] * coef for i in range(r)], axis=0)
    ones = valid_ref[...].astype(BF16)
    flat = sum(lax.dot_general(ones, part, NT, preferred_element_type=F32) for part in split3(products))
    lane = lax.broadcasted_iota(jnp.int32, flat.shape, 1)
    flat = jnp.where(lane == sz.spot, total, flat)
    for at in range(0, note_ref.shape[0], 8):
        note_ref[at : at + 8, :] = flat


def invert_gram(sz, note_ref, inverse_ref):
    r = sz.rank
    flat = jnp.sum(note_ref[...], axis=0, keepdims=True)
    gram = jnp.concatenate([flat[:, i * r : (i + 1) * r] for i in range(r)], axis=0)
    row = lax.broadcasted_iota(jnp.int32, (r, r), 0)
    col = lax.broadcasted_iota(jnp.int32, (r, r), 1)
    twin = flat[:, sz.twin : sz.twin + 1]
    gram = jnp.where((row == r - 1) & (col == r - 2), twin, gram)
    gram = gram / (sz.n_pix * sz.tiles_all) + RIDGE * eye_at((r, r), 0)
    (inverse_ref[...],) = solve_spd(gram, [eye_at((r, BLOCK), 0)])


def update_terms(sz, width, ks, note_ref, f_ref, bar_ref, three_ref, parts_ref, *refs):
    r = sz.rank
    total = jnp.sum(note_ref[:, sz.spot : sz.spot + 1], axis=0, keepdims=True)
    spread = total / (sz.tiles_all * sz.pixels_all) + 1e-05
    scale = jnp.broadcast_to(1.0 / (4.0 * spread), (8, BLOCK))[0:1, :]
    for k, stack_ref, out_ref in zip(ks, refs[: len(ks)], refs[len(ks) :]):
        chunk_terms(sz, width, k, scale, f_ref, stack_ref, bar_ref, three_ref, parts_ref, out_ref)


def chunk_terms(sz, width, k, scale, f_ref, stack_ref, bar_ref, three_ref, parts_ref, out_ref):
    r = sz.rank
    start = start_of(sz, k)
    parts = parts_ref[:, 0 : sz.stack]
    three = three_ref[...]
    two = three[0 : 2 * r + 16]
    each = width // BLOCK

    def place(flat):
        lane = sz.chunk + flat // r * BLOCK
        return slice(flat % r, flat % r + 1), slice(lane, lane + BLOCK)

    for step in range(sz.chunk // width):
        res = residual(sz, f_ref, stack_ref, parts, start, step, width)
        hi_parts, mid_parts = [], []
        for j in range(each):
            block = (start // BLOCK + step * each + j) % (ROW_PX // BLOCK)
            x = res[:, j * BLOCK : (j + 1) * BLOCK]
            g = pl.reciprocal(x * x * scale + bar_ref[jnp.minimum(block, bar_ref.shape[0] - 1)], approx=True)
            out_ref[place(sz.blocks + step * each + j)] = jnp.sum(g, axis=0, keepdims=True)
            w = g * x
            w_hi = w.astype(BF16)
            hi_parts.append(w_hi)
            mid_parts.append((w - w_hi.astype(F32)).astype(BF16))
        terms = lax.dot_general(three, jnp.concatenate(hi_parts, axis=1), NN, preferred_element_type=F32)
        more = lax.dot_general(two, jnp.concatenate(mid_parts, axis=1), NN, preferred_element_type=F32)
        out_ref[:, step * width : (step + 1) * width] = terms[0:r] + (
            terms[r : 2 * r] + terms[2 * r + 16 :] + more[0:r] + more[r : 2 * r]
        )
        sums = terms[2 * r : 2 * r + 1] + more[2 * r : 2 * r + 1]
        for j in range(each):
            out_ref[place(step * each + j)] = sums[:, j * BLOCK : (j + 1) * BLOCK]
    used = 2 * sz.blocks
    if used % r:
        out_ref[used % r :, sz.chunk + used // r * BLOCK :] = jnp.zeros((r - used % r, BLOCK), F32)


def update_chunk(sz, places, inverse_ref, old_ref, *refs):
    total_refs, new_ref = refs[:-1], refs[-1]
    r = sz.rank
    totals = tree([total_refs[i][...] for i in places])
    inverse = inverse_ref[:, 0:r]
    change = jnp.dot(inverse, totals[:, 0 : sz.chunk] / sz.tiles_all, precision=lax.Precision.HIGHEST, preferred_element_type=F32)
    new_ref[:, 0 : sz.chunk] = old_ref[:, 0 : sz.chunk] + change
    new_ref[:, sz.chunk :] = jnp.zeros((r, sz.extra), F32)

    def place(flat):
        return flat % r, sz.chunk + flat // r * BLOCK

    many = 8 if sz.blocks % 8 == 0 else 1
    for j in range(0, sz.blocks, many):
        (row, lane), (row_g, lane_g) = place(j), place(sz.blocks + j)
        w = totals[row : row + many, lane : lane + BLOCK]
        g = totals[row_g : row_g + many, lane_g : lane_g + BLOCK]
        new_ref[row : row + many, lane : lane + BLOCK] = (
            old_ref[row : row + many, lane : lane + BLOCK] + w / (g + 1.0)
        )


def assemble(sz, ks, coef_ref, *refs):
    chunks, (b_ref, d_ref, coef_out_ref) = refs[: sz.group], refs[sz.group :]
    coef_out_ref[...] = coef_ref[...]
    me = lax.axis_index("tiles") & (sz.group - 1)
    for k, ref in zip(ks, chunks):
        c = me ^ k
        b_ref[:, pl.ds(pl.multiple_of(c * sz.chunk, BLOCK), sz.chunk)] = ref[:, 0 : sz.chunk]
        for j in range(sz.blocks):
            lane = sz.chunk + j // sz.rank * BLOCK
            d_ref[c * sz.blocks + j, :] = ref[j % sz.rank, lane : lane + BLOCK]


def call(body, outs, ins, in_hbm=False, scratch=()):
    return pl.pallas_call(
        body,
        out_shape=[jax.ShapeDtypeStruct(s, t) for s, t in outs],
        in_specs=[pl.BlockSpec(memory_space=pltpu.HBM)] * len(ins) if in_hbm else vmem(len(ins)),
        out_specs=vmem(len(outs)),
        scratch_shapes=scratch,
        compiler_params=params(),
    )(*([pltpu.with_memory_space_constraint(x, pltpu.HBM) for x in ins] if in_hbm else ins))


def local(frames, tile_valid, foreground_blocks, basis_start, dark_start):
    td, pd = frames.shape
    r = basis_start.shape[0]
    sz = Sizes(td, pd, r, lax.axis_size("tiles"), lax.axis_size("pix"))
    everyone = ("tiles", "pix")
    devices = sz.n_tiles * sz.n_pix
    pix_masks = range(1, sz.n_pix)
    width = min(256, sz.chunk)
    chunk_shape = (r, sz.chunk + sz.extra)
    packed_out = ((r, td + BLOCK), F32)
    stack_out = ((sz.stack, sz.chunk), BF16)
    masks = sz.tile_levels[0]
    for iteration in range(ITERS):
        if iteration == 0:
            frames, packed, old, least, valid, *stacks = call(
                functools.partial(first_projection, sz),
                [((td, pd), BF16), packed_out, (chunk_shape, F32), ((8, td), jnp.int32), ((8, td), F32)]
                + [stack_out] * sz.group,
                [frames, basis_start, dark_start.reshape(pd // BLOCK, BLOCK), tile_valid.reshape(1, td), foreground_blocks.reshape(1, td)],
                in_hbm=True,
                scratch=[
                    pltpu.VMEM((r, pd), F32),
                    pltpu.VMEM((pd // BLOCK, BLOCK), F32),
                    pltpu.VMEM((16, td), jnp.int32),
                    pltpu.SemaphoreType.DMA((4 + sz.group,)),
                ],
            )
        else:
            before, stacks = [], [None] * sz.group
            for k in [0] + permuted(masks, ORDER[2]):
                packed, stacks[k] = call(
                    functools.partial(later_projection, sz, k), [packed_out, stack_out], [frames, chunks[k]] + before
                )
                before = [packed]
        if iteration == 0:
            mask = ((ROW_PX // BLOCK // 2 + 1, td, BLOCK), F32)
            keep, bar = call(make_masks, [mask, mask], [least])
        both = [packed] + [partner(packed, "pix", m) for m in pix_masks]
        coef, three, parts, note = call(
            functools.partial(solve_tiles, sz, width),
            [((r, td), F32), ((3 * r + 16, td), BF16), ((td, BLOCK), BF16), ((devices, r * r), F32)],
            both + stacks + [frames, keep, valid],
        )
        notes = lax.all_to_all(note, everyone, 0, 0, tiled=True)
        (inverse,) = call(functools.partial(invert_gram, sz), [((r, BLOCK), F32)], [notes])
        terms = {}
        for ks in (list(masks), [0]):
            outs = call(
                functools.partial(update_terms, sz, width, ks),
                [(chunk_shape, F32)] * len(ks),
                [notes, frames, bar, three, parts] + [stacks[k] for k in ks],
            )
            terms.update(zip(ks, outs))
        order = permuted(masks, ORDER[0])
        got = dict(zip(order, lax.optimization_barrier([partner(terms[m], "tiles", m) for m in order])))
        total = tree([terms[0]] + [got[m] for m in masks])
        later = sz.tile_levels[1:]
        for level in later[:-1]:
            total = sum_level(total, "tiles", level)
        last = later[-1] if later else ()
        order = permuted(last, ORDER[1])
        swap = {last[0]: last[1], last[1]: last[0]} if len(last) == 3 else {}
        totals = [total] + [crossed(total, m, swap) for m in order]
        places = [0] + [1 + order.index(m) for m in last]
        (old,) = call(functools.partial(update_chunk, sz, places), [(chunk_shape, F32)], [inverse, old] + totals)
        chunks = [old] + [partner(old, "tiles", m) for m in masks]
    ks = [0] + permuted(masks, ORDER[3])
    basis, dark, coef = call(
        functools.partial(assemble, sz, ks),
        [((r, pd), F32), ((pd // BLOCK, BLOCK), F32), ((r, td), F32)],
        [coef] + [chunks[k] for k in ks],
    )
    return basis, dark.reshape(pd), coef.T


def solution(mesh):
    return jax.shard_map(
        local,
        mesh=mesh,
        in_specs=(P("tiles", "pix"), P("tiles"), P("tiles"), P(None, "pix"), P("pix")),
        out_specs=(P(None, "pix"), P("pix"), P("tiles", None)),
        check_vma=False,
    )
```
